32 devices in a mesh: gx: 4 (over z), gy: 8 (over y, x, core).
Axes of the slice: x: 2, y: 2, z: 4, core: 2. Of those that a mesh axis runs over, the one named last changes fastest.
Arguments:
- positions: float32 [3, 524288], P(None, ('gx', 'gy')), may hold values from -0.5 to 0.5, as said below
- charges: float32 [524288], P(('gx', 'gy')), may hold values from -0.36 to 0.36
- near_leaves: int32 [4096, 27], P(('gx', 'gy')), may hold values from -1 to 4095, as said below
- near_offsets: int32 [4096, 27], P(('gx', 'gy')), may hold values from 0 to 26, as said below
- far_leaves: int32 [4096, 189], P(('gx', 'gy')), may hold values from -1 to 639, as said below
- far_leaf_class: int32 [4096, 189], P(('gx', 'gy')), may hold values from 0 to 15
- leaf_plan: int32 [32, 32, 16], P(('gx', 'gy')), may hold values from -1 to 127, as said below
- far_parents: int32 [512, 189], P(('gx', 'gy')), may hold values from -1 to 143, as said below
- far_parent_class: int32 [512, 189], P(('gx', 'gy')), may hold values from 0 to 15
- parent_plan: int32 [32, 32, 4], P(('gx', 'gy')), may hold values from -1 to 15, as said below
- coarse_lists: int32 [8, 7], replicated, may hold values from 0 to 7, as said below
- coarse_class: int32 [8, 7], replicated, may hold values from 0 to 15
- up_shift: float32 [8, 286, 286], replicated, may hold values from -4 to 4
- down_shift: float32 [8, 286, 286], replicated, may hold values from -4 to 4
- far_shift: float32 [16, 286, 286], replicated, may hold values from -2 to 2
Outputs:
- potential: float32 [524288], P(('gx', 'gy'))
The draws below stay inside these ranges and needn't reach their ends.
Inputs may be any that keep to these rules, and one draw needn't show every extreme that they name: `positions`: each coordinate lies within half a leaf width of its leaf centre. `near_leaves`: entry 0 of every list is the leaf itself with offset class 13; the other entries name leaves at most 32 before the first leaf or after the last leaf of the list's own device; -1 pads a list's tail. `near_offsets`: entry 0 is 13. `leaf_plan`: row d, column o lists distinct local indices of leaves of device o that device d names, then -1; at most 16 a pair, reached in every draw; a device names none of its own. `far_leaves`: slots name only own leaves or filled entries of the device's row of leaf_plan; -1 pads a list's tail. `parent_plan`: as leaf_plan, for parent cells, at most 4 a pair, reached in every draw. `far_parents`: slots name only own parents or filled entries of the device's row of parent_plan; -1 pads a list's tail. `coarse_lists`: each row names distinct cells other than its own.
All inputs are finite; a program needn't handle non-finite values.
Results may differ from the reference program's by a relative error of at most 0.0003.
Values sent between devices are 32-bit elements; how exact they have to be, the bound alone decides.
A program may use at most 192 MiB of HBM per device.

```python
import math
import jax
import jax.numpy as jnp
import numpy as np
from jax import lax

ORDER = 10
COEF = 286
LEAF_SIZE = 128
LEAF_DEV = 128
K_NEAR = 27
K_FAR = 189
K_COARSE = 7
OFFSETS = 16
CAP_L = 16
CAP_P = 4
RIM = 32
P_DEV = 16
LEAVES = 4096
PARENTS = 512
NCOARSE = 8
PARTICLES = 524288


def degree_table(order):
    spreads = []
    for degree in range(order + 1):
        for first_power in range(degree, -1, -1):
            for second_power in range(degree - first_power, -1, -1):
                third_power = degree - first_power - second_power
                product = (2 * first_power + 1) * (2 * second_power + 1) * (2 * third_power + 1)
                spreads.append(1.0 / math.sqrt(product))
    return jnp.asarray(np.array(spreads, dtype=np.float32))


def draw_positions(key, part):
    key = jax.random.fold_in(key, 41)
    return jax.random.uniform(key, (3, PARTICLES), jnp.float32, -0.5, 0.5)


def draw_up_shift(key, part):
    key = jax.random.fold_in(key, 42)
    scales = degree_table(ORDER)
    entries = jax.random.truncated_normal(key, -3.0, 3.0, (8, COEF, COEF), jnp.float32)
    return entries * (scales[None, :, None] / scales[None, None, :]) * (8.0 * COEF) ** (-0.5)


def draw_down_shift(key, part):
    key = jax.random.fold_in(key, 43)
    scales = degree_table(ORDER)
    entries = jax.random.truncated_normal(key, -3.0, 3.0, (8, COEF, COEF), jnp.float32)
    return entries * (scales[None, None, :] / scales[None, :, None]) * (1.0 * COEF) ** (-0.5)


def draw_far_shift(key, part):
    key = jax.random.fold_in(key, 44)
    scales = degree_table(ORDER)
    entries = jax.random.truncated_normal(key, -3.0, 3.0, (OFFSETS, COEF, COEF), jnp.float32)
    return entries / (scales[None, :, None] * scales[None, None, :]) * (1.0 * COEF * COEF * K_FAR) ** (-0.5)


def let_plan(key, salt, cells_dev, capacity, list_width):
    key = jax.random.fold_in(key, salt)
    device_count = LEAVES // LEAF_DEV
    keys = jax.random.split(key, 6)
    device_range = jnp.arange(device_count, dtype=jnp.int32)
    counts = jax.random.randint(keys[0], (device_count, device_count), 1, capacity + 1)
    stride = jax.random.randint(keys[1], (device_count,), 1, device_count)
    stride = stride.at[0].set(device_count - 1)
    fullest = (device_range + stride) % device_count
    counts = jnp.where(device_range[None, :] == fullest[:, None], capacity, counts)
    counts = jnp.where(device_range[None, :] == device_range[:, None], 0, counts)
    scores = jax.random.randint(keys[2], (device_count, device_count, cells_dev), 0, 1 << 20) * cells_dev + jnp.arange(cells_dev, dtype=jnp.int32)
    scores = scores.at[0, device_count - 1, cells_dev - 1].set(-1)
    ranking = jnp.argsort(scores, axis=-1)[:, :, :capacity].astype(jnp.int32)
    plan = jnp.where(jnp.arange(capacity, dtype=jnp.int32) < counts[:, :, None], ranking, -1)
    owner = jax.random.randint(keys[3], (device_count, cells_dev, list_width), 0, device_count)
    owner = owner.at[0, 0, 1].set(device_count - 1)
    picks = jax.random.randint(keys[4], (device_count, cells_dev, list_width), 0, 1 << 20)
    picks = picks.at[0, 0, 1].set(capacity - 1)
    own_cell = owner == device_range[:, None, None]
    available = counts[device_range[:, None, None], owner]
    chosen = picks % jnp.where(own_cell, cells_dev, jnp.maximum(available, 1))
    slots = jnp.where(own_cell, chosen, cells_dev + owner * capacity + chosen)
    filled = jax.random.randint(keys[5], (device_count, cells_dev), list_width // 2, list_width + 1)
    filled = filled.at[:, 0].set(list_width).at[0, 1].set(list_width // 2)
    slots = jnp.where(jnp.arange(list_width, dtype=jnp.int32) < filled[:, :, None], slots, -1)
    return (plan.astype(jnp.int32), slots.reshape(device_count * cells_dev, list_width).astype(jnp.int32))


def draw_leaf_plan(key, part):
    return let_plan(key, 11, LEAF_DEV, CAP_L, K_FAR)[0]


def draw_far_leaves(key, part):
    return let_plan(key, 11, LEAF_DEV, CAP_L, K_FAR)[1]


def draw_parent_plan(key, part):
    return let_plan(key, 12, P_DEV, CAP_P, K_FAR)[0]


def draw_far_parents(key, part):
    return let_plan(key, 12, P_DEV, CAP_P, K_FAR)[1]


def draw_near_leaves(key, part):
    key = jax.random.fold_in(key, 21)
    keys = jax.random.split(key, 2)
    leaf_ids = jnp.arange(LEAVES, dtype=jnp.int32)
    owner = leaf_ids // LEAF_DEV
    lowest = jnp.maximum(owner * LEAF_DEV - RIM, 0)
    highest_leaf = jnp.minimum((owner + 1) * LEAF_DEV + RIM, LEAVES)
    picks = jax.random.randint(keys[0], (LEAVES, K_NEAR), 0, 1 << 20)
    named = lowest[:, None] + picks % (highest_leaf - lowest)[:, None]
    first_leaf = leaf_ids % LEAF_DEV == 0
    last_leaf = leaf_ids % LEAF_DEV == LEAF_DEV - 1
    reach = jnp.where(first_leaf, owner * LEAF_DEV - RIM, jnp.where(last_leaf, (owner + 1) * LEAF_DEV + RIM - 1, named[:, 1]))
    reach = jnp.clip(reach, 0, LEAVES - 1)
    named = named.at[:, 1].set(reach).at[:, 0].set(leaf_ids)
    filled = jax.random.randint(keys[1], (LEAVES,), 8, K_NEAR + 1)
    filled = filled.at[1].set(8)
    return jnp.where(jnp.arange(K_NEAR, dtype=jnp.int32) < filled[:, None], named, -1).astype(jnp.int32)


def draw_near_offsets(key, part):
    key = jax.random.fold_in(key, 22)
    classes = jax.random.randint(key, (LEAVES, K_NEAR), 0, 27)
    return classes.at[:, 0].set(13).astype(jnp.int32)


def draw_coarse_lists(key, part):
    key = jax.random.fold_in(key, 31)
    scores = jax.random.randint(key, (NCOARSE, NCOARSE - 1), 0, 1 << 20) * (NCOARSE - 1) + jnp.arange(NCOARSE - 1, dtype=jnp.int32)
    scores = scores.at[0, NCOARSE - 2].set(-1).at[NCOARSE - 1, 0].set(-1)
    ranking = jnp.argsort(scores, axis=-1)[:, :K_COARSE].astype(jnp.int32)
    return ((jnp.arange(NCOARSE, dtype=jnp.int32)[:, None] + 1 + ranking) % NCOARSE).astype(jnp.int32)


def place_ends(drawn, stream_key, low, top_value):
    longest = drawn.shape.index(max(drawn.shape))
    spots = []
    for shift in (0, 1):
        where = [jax.random.randint(jax.random.fold_in(stream_key, axis), (), 0, length) for axis, length in enumerate(drawn.shape)]
        where[longest] = (where[longest] + shift) % drawn.shape[longest]
        spots.append(tuple(where))
    return drawn.at[spots[0]].set(low).at[spots[1]].set(top_value)


def levels(key, dims, cuts, smallest, top_value):
    def one(dim, parts):
        heights = jax.random.uniform(jax.random.fold_in(jax.random.fold_in(key, 6), dim), (parts,), jnp.float32, smallest / len(cuts), top_value / len(cuts))
        return jnp.repeat(jnp.exp(heights), dims[dim] // parts).reshape((-1,) + (1,) * (len(dims) - dim - 1))

    loudness = one(*cuts[0])
    for cut in cuts[1:]:
        loudness = loudness * one(*cut)
    return loudness


def scatter_about(key, shape, scale, most, cuts=(), held_as=jnp.bfloat16):
    values = scale * jax.random.normal(key, shape, jnp.float32)
    if cuts:
        values = values * levels(key, shape, cuts, -0.22, 0.18)
    return jnp.clip(values, -most, most).astype(held_as)


def setup_inputs(seed: int = 0) -> dict:
    key_list = jax.random.split(jax.random.key(seed), 16)
    positions = draw_positions(jax.random.fold_in(key_list[15], 71), 0)
    charges = scatter_about(key_list[1], (PARTICLES,), 0.06, 0.36, ((0, 32),), jnp.float32)
    near_leaves = draw_near_leaves(jax.random.fold_in(key_list[15], 71), 0)
    near_offsets = draw_near_offsets(jax.random.fold_in(key_list[15], 71), 0)
    far_leaves = draw_far_leaves(jax.random.fold_in(key_list[15], 71), 0)
    far_leaf_class = place_ends(jax.random.randint(key_list[5], (LEAVES, K_FAR), 0, OFFSETS), jax.random.fold_in(key_list[5], 1), 0, OFFSETS - 1).astype(jnp.int32)
    leaf_plan = draw_leaf_plan(jax.random.fold_in(key_list[15], 71), 0)
    far_parents = draw_far_parents(jax.random.fold_in(key_list[15], 71), 0)
    far_parent_class = place_ends(jax.random.randint(key_list[8], (PARENTS, K_FAR), 0, OFFSETS), jax.random.fold_in(key_list[8], 1), 0, OFFSETS - 1).astype(jnp.int32)
    parent_plan = draw_parent_plan(jax.random.fold_in(key_list[15], 71), 0)
    coarse_lists = draw_coarse_lists(jax.random.fold_in(key_list[15], 71), 0)
    coarse_class = place_ends(jax.random.randint(key_list[11], (NCOARSE, K_COARSE), 0, OFFSETS), jax.random.fold_in(key_list[11], 1), 0, OFFSETS - 1).astype(jnp.int32)
    up_shift = draw_up_shift(jax.random.fold_in(key_list[15], 71), 0)
    down_shift = draw_down_shift(jax.random.fold_in(key_list[15], 71), 0)
    far_shift = draw_far_shift(jax.random.fold_in(key_list[15], 71), 0)
    return dict(positions=positions, charges=charges, near_leaves=near_leaves, near_offsets=near_offsets, far_leaves=far_leaves, far_leaf_class=far_leaf_class, leaf_plan=leaf_plan, far_parents=far_parents, far_parent_class=far_parent_class, parent_plan=parent_plan, coarse_lists=coarse_lists, coarse_class=coarse_class, up_shift=up_shift, down_shift=down_shift, far_shift=far_shift)


softening = 0.05
highest = lax.Precision.HIGHEST

def exponents(order):
    entries = []
    for degree in range(order + 1):
        for first_power in range(degree, -1, -1):
            for second_power in range(degree - first_power, -1, -1):
                entries.append((first_power, second_power, degree - first_power - second_power))
    return np.array(entries, dtype=np.int32).T

def basis(coords):
    scaled = 2.0 * coords
    powers = [jnp.ones_like(scaled)]
    for degree in range(ORDER):
        powers.append(powers[-1] * scaled)
    stacked = jnp.stack(powers)
    exponent_table = exponents(ORDER)
    return stacked[exponent_table[0], 0] * stacked[exponent_table[1], 1] * stacked[exponent_table[2], 2]

def upward(children, up_shift):
    grouped = children.reshape(children.shape[0], -1, 8)
    return jnp.einsum('cab,bnc->an', up_shift, grouped, precision=highest)

def downward(parents, down_shift):
    spread = jnp.einsum('cab,bn->anc', down_shift, parents, precision=highest)
    return spread.reshape(spread.shape[0], -1)

def far_field(sources, slots, classes, far_shift, block):
    targets, list_width = slots.shape
    operator_count = far_shift.shape[0]

    def one_block(pieces):
        slot_block, class_block = pieces
        present = slot_block >= 0
        columns = sources[:, jnp.maximum(slot_block, 0)]
        selector = ((class_block[..., None] == jnp.arange(operator_count, dtype=jnp.int32)) & present[..., None]).astype(jnp.float32)
        grouped = jnp.einsum('ctk,tko->otc', columns, selector, precision=highest)
        return jnp.einsum('oac,otc->at', far_shift, grouped, precision=highest)
    if targets <= block:
        return one_block((slots, classes))
    results = lax.map(one_block, (slots.reshape(-1, block, list_width), classes.reshape(-1, block, list_width)))
    return jnp.moveaxis(results, 0, 1).reshape(sources.shape[0], targets)

def near_sum(sources, targets, source_index, present, near_leaves, near_offsets, target_ids):
    leaf_count, leaf_size = (targets.shape[1], targets.shape[2])
    diagonal = jnp.eye(leaf_size, dtype=bool)

    def add_slot(entry_slot, running):
        source_rows = lax.dynamic_index_in_dim(source_index, entry_slot, 1, keepdims=False)
        neighbour = lax.dynamic_index_in_dim(near_leaves, entry_slot, 1, keepdims=False)
        counted_slot = lax.dynamic_index_in_dim(present, entry_slot, 1, keepdims=False)
        offset_class = lax.dynamic_index_in_dim(near_offsets, entry_slot, 1, keepdims=False)
        gathered = sources[:, source_rows]
        shift_x = (offset_class // 9 - 1).astype(jnp.float32)
        shift_y = (offset_class // 3 % 3 - 1).astype(jnp.float32)
        shift_z = (offset_class % 3 - 1).astype(jnp.float32)
        step_x = gathered[0][:, None, :] + shift_x[:, None, None] - targets[0][:, :, None]
        step_y = gathered[1][:, None, :] + shift_y[:, None, None] - targets[1][:, :, None]
        step_z = gathered[2][:, None, :] + shift_z[:, None, None] - targets[2][:, :, None]
        squared = step_x * step_x + step_y * step_y + step_z * step_z + softening * softening
        itself = (neighbour == target_ids) & (offset_class == 13)
        counted = counted_slot[:, None, None] & jnp.logical_not(itself[:, None, None] & diagonal[None])
        contributions = jnp.where(counted, gathered[3][:, None, :] * lax.rsqrt(squared), 0.0)
        return running + lax.optimization_barrier(jnp.sum(contributions, axis=2))
    return lax.fori_loop(0, near_leaves.shape[1], add_slot, jnp.zeros((leaf_count, leaf_size), jnp.float32))

def decode(slots, plan, cells_dev):
    capacity = plan.shape[2]
    owner_row = (jnp.arange(slots.shape[0], dtype=jnp.int32) // cells_dev)[:, None]
    ghost = jnp.maximum(slots - cells_dev, 0)
    owner = ghost // capacity
    position = ghost % capacity
    remote = owner * cells_dev + plan[owner_row, owner, position]
    return jnp.where(slots < 0, -1, jnp.where(slots < cells_dev, owner_row * cells_dev + slots, remote))

def reference(positions, charges, near_leaves, near_offsets, far_leaves, far_leaf_class, leaf_plan, far_parents, far_parent_class, parent_plan, coarse_lists, coarse_class, up_shift, down_shift, far_shift):
    coef_count = up_shift.shape[1]
    blocks = LEAVES // 512
    span = 512 * LEAF_SIZE
    coords = jnp.moveaxis(positions.reshape(3, blocks, span), 1, 0)
    weights = charges.reshape(blocks, span)

    def moments(pieces):
        block_coords, block_weights = pieces
        return (basis(block_coords) * block_weights).reshape(coef_count, 512, LEAF_SIZE).sum(axis=2)
    leaf_multipoles = jnp.moveaxis(lax.map(moments, (coords, weights)), 0, 1).reshape(coef_count, LEAVES)
    parent_multipoles = upward(leaf_multipoles, up_shift)
    grand_multipoles = upward(parent_multipoles, up_shift)
    coarse_multipoles = upward(grand_multipoles, up_shift)
    coarse_locals = far_field(coarse_multipoles, coarse_lists, coarse_class, far_shift, 256)
    grand_locals = downward(coarse_locals, down_shift)
    source_parent = decode(far_parents, parent_plan, P_DEV)
    parent_locals = downward(grand_locals, down_shift) + far_field(parent_multipoles, source_parent, far_parent_class, far_shift, 256)
    source_leaf = decode(far_leaves, leaf_plan, LEAF_DEV)
    leaf_locals = downward(parent_locals, down_shift) + far_field(leaf_multipoles, source_leaf, far_leaf_class, far_shift, 256)
    local_blocks = jnp.moveaxis(leaf_locals.reshape(coef_count, blocks, 512), 1, 0)

    def evaluate(pieces):
        block_coords, block_locals = pieces
        values = basis(block_coords).reshape(coef_count, 512, LEAF_SIZE)
        return jnp.einsum('alp,al->lp', values, block_locals, precision=highest)
    far_potential = lax.map(evaluate, (coords, local_blocks))
    particle_data = jnp.concatenate([positions, charges[None]], 0).reshape(4, LEAVES, LEAF_SIZE)

    def near_block(index):
        start = (index * 512).astype(jnp.int32)
        targets = lax.dynamic_slice_in_dim(particle_data, start, 512, 1)
        rows = lax.dynamic_slice_in_dim(near_leaves, start, 512, 0)
        offsets = lax.dynamic_slice_in_dim(near_offsets, start, 512, 0)
        target_ids = start + jnp.arange(512, dtype=jnp.int32)
        return near_sum(particle_data, targets, jnp.maximum(rows, 0), rows >= 0, rows, offsets, target_ids)
    near_potential = lax.map(near_block, jnp.arange(blocks, dtype=jnp.int32))
    return near_potential.reshape(-1) + far_potential.reshape(-1)
```

```python
import functools

import jax
import jax.numpy as jnp
from jax import lax
from jax.experimental import pallas as pl
from jax.experimental.pallas import tpu as pltpu
from jax.sharding import PartitionSpec as P

ORDER = 10
RIM = 32
QUAD = 4
softening = 0.05
AXES = ("gx", "gy")
VMEM_LIMIT = 56 * 1024 * 1024
f32 = jnp.float32
bf16 = jnp.bfloat16


def exponent_index(order):
    index = {}
    for degree in range(order + 1):
        for i in range(degree, -1, -1):
            for j in range(degree - i, -1, -1):
                index[(i, j, degree - i - j)] = len(index)
    return index


INDEX = exponent_index(ORDER)
NT = (((1,), (1,)), ((), ()))


def split2(x):
    high = x.astype(bf16)
    low = (x - high.astype(f32)).astype(bf16)
    return high, low


def dot_nt(x, w):
    xh, xl = split2(x)
    wh, wl = split2(w)
    out = lax.dot_general(xh, wh, NT, preferred_element_type=f32)
    out += lax.dot_general(xl, wh, NT, preferred_element_type=f32)
    return out + lax.dot_general(xh, wl, NT, preferred_element_type=f32)


def joined(held, rows, coef):
    return jnp.concatenate([held[b, rows, :] for b in range(held.shape[0])], axis=1)[:, :coef]


def spread_to(held, rows, value):
    value = jnp.pad(value, ((0, 0), (0, held.shape[0] * 128 - value.shape[1])))
    for b in range(held.shape[0]):
        held[b, rows, :] = value[:, b * 128 : (b + 1) * 128]


def upward_kernel(ids_ref, pos_ref, chg_ref, up_ref, leaf_ref, parent_ref, lifted_ref, mom, rows, prow):
    coef = up_ref.shape[1]
    parents = parent_ref.shape[0]
    grands = parents // 8
    mom[...] = jnp.zeros_like(mom)
    xt = pos_ref[0].T * 2.0
    yt = pos_ref[1].T * 2.0
    zt = pos_ref[2].T * 2.0
    qt = chg_ref[...].T
    size = xt.shape[0]
    chunk = 64
    for start in range(0, size, chunk):
        x, y, z, wi = (v[start : start + chunk] for v in (xt, yt, zt, qt))
        for i in range(ORDER + 1):
            if i:
                wi = wi * x
            wj = wi
            for j in range(ORDER + 1 - i):
                if j:
                    wj = wj * y
                wk = wj
                for k in range(ORDER + 1 - i - j):
                    if k:
                        wk = wk * z
                    a = INDEX[(i, j, k)]
                    mom[a : a + 1, :] += jnp.sum(wk, axis=0, keepdims=True)
    for b in range(mom.shape[0] // 128):
        rows[b] = mom[b * 128 : (b + 1) * 128, :].T
    leaf_ref[...] = joined(rows, slice(None), coef)
    total = jnp.zeros((parents, coef), f32)
    for c in range(8):
        total += dot_nt(joined(rows, pl.ds(c, parents, stride=8), coef), up_ref[c])
    parent_ref[...] = total
    spread_to(prow, slice(None), total)
    grand = jnp.zeros((grands, coef), f32)
    for c in range(8):
        grand += dot_nt(joined(prow, pl.ds(c, grands, stride=8), coef), up_ref[c])
    for g in range(grands):
        lifted_ref[g : g + 1, :] = dot_nt(grand[g : g + 1], up_ref[ids_ref[g]])


def upward_call(ids, pos, chg, up):
    leaves = pos.shape[1]
    coef = up.shape[1]
    parents = leaves // 8
    wide = pl.cdiv(coef, 128) * 128
    vmem = pl.BlockSpec(memory_space=pltpu.VMEM)
    return pl.pallas_call(
        upward_kernel,
        out_shape=(
            jax.ShapeDtypeStruct((leaves, coef), f32),
            jax.ShapeDtypeStruct((parents, coef), f32),
            jax.ShapeDtypeStruct((parents // 8, coef), f32),
        ),
        in_specs=[pl.BlockSpec(memory_space=pltpu.SMEM), vmem, vmem, vmem],
        out_specs=(vmem, vmem, vmem),
        scratch_shapes=[
            pltpu.VMEM((wide, leaves), f32),
            pltpu.VMEM((wide // 128, leaves, 128), f32),
            pltpu.VMEM((wide // 128, parents, 128), f32),
        ],
        compiler_params=pltpu.CompilerParams(vmem_limit_bytes=VMEM_LIMIT),
        name="upward",
    )(ids, pos, chg, up)


def near_kernel(
    leaves, width, count_ref, src_ref, off_ref, total_ref, data_ref, table_ref, out_ref,
    targets, acc, b0, b1, r0, r1,
):
    row = lax.broadcasted_iota(jnp.int32, (8, 128), 0)
    soft = softening * softening

    def pieces(s):
        p1 = s.astype(bf16).astype(f32)
        rest = s - p1
        p2 = rest.astype(bf16).astype(f32)
        return p1, p2, rest - p2

    def set_target(l, carry):
        t = data_ref[RIM + l]
        square = jnp.sum(jnp.where(row < 3, t * t, 0.0), axis=0, keepdims=True)
        t = jnp.where(row < 3, -2.0 * t, jnp.where(row == 3, 1.0, jnp.where(row == 4, square, 0.0)))
        t1, t2, t3 = pieces(t)
        zero = jnp.zeros((80, 128), f32)
        full = jnp.concatenate([t1, t2, t3, t1, t2, t1, zero], axis=0)
        targets[l] = full.T[:, :48].astype(bf16)
        acc[l] = jnp.zeros((128, 128), f32)
        return carry

    lax.fori_loop(0, leaves, set_target, 0, unroll=4)

    def build(l, k, b):
        named = []
        for j in range(QUAD):
            entry = l * width + k + j
            m = src_ref[entry]
            s = data_ref[m] + table_ref[off_ref[entry]]
            square = jnp.sum(jnp.where(row < 3, s * s, 0.0), axis=0, keepdims=True) + soft
            s = jnp.where(row == 3, square, s)
            s1, s2, s3 = pieces(s)
            b[:, j * 128 : (j + 1) * 128] = jnp.concatenate([s1, s1, s1, s2, s2, s3], axis=0).astype(bf16)
            named.append(m)
        return tuple(named)

    def multiply(l, b, r):
        r[...] = jnp.dot(targets[jnp.minimum(l, leaves - 1)], b[...], preferred_element_type=f32)

    def collect(l, named, r):
        charges = [data_ref[m, 5:6, :] for m in named]
        for start in range(0, 128, 32):
            part = acc[l, start : start + 32, :]
            for j in range(QUAD):
                part += lax.rsqrt(r[start : start + 32, j * 128 : (j + 1) * 128]) * charges[j]
            acc[l, start : start + 32, :] = part

    def step(state, b_new, b_old, r_new, r_old):
        l, k, l1, named1, l2, named2 = state
        collect(l2, named2, r_old)
        multiply(l1, b_old, r_new)
        named = build(l, k, b_new)
        more = k + QUAD < count_ref[l]
        k_next = jnp.where(more, k + QUAD, 0)
        l_next = jnp.where(more, l, jnp.minimum(l + 1, leaves))
        return l_next, k_next, l, named, l1, named1

    def both(it, state):
        state = step(state, b0, b1, r1, r0)
        return step(state, b1, b0, r0, r1)

    none = jnp.int32(leaves)
    empty = (jnp.int32(data_ref.shape[0] - 1),) * QUAD
    start = (jnp.int32(0), jnp.int32(0), none, empty, none, empty)
    lax.fori_loop(0, (total_ref[0] + 3) // 2, both, start)

    lane = lax.broadcasted_iota(jnp.int32, (128, 128), 1)
    out_ref[...] = jnp.zeros_like(out_ref)

    def finish(l, carry):
        total = jnp.sum(acc[l], axis=1, keepdims=True)
        out_ref[...] = jnp.where(lane == l, total, out_ref[...])
        return carry

    lax.fori_loop(0, leaves, finish, 0, unroll=8)


def near_call(counts, sources, offsets, total, data, table, leaves, width):
    vmem = pl.BlockSpec(memory_space=pltpu.VMEM)
    smem = pl.BlockSpec(memory_space=pltpu.SMEM)
    pairs = leaves * 18 * 128 * 128
    return pl.pallas_call(
        functools.partial(near_kernel, leaves, width),
        out_shape=jax.ShapeDtypeStruct((128, leaves), f32),
        in_specs=[smem, smem, smem, smem, vmem, vmem],
        out_specs=vmem,
        scratch_shapes=[
            pltpu.VMEM((leaves, 128, 48), bf16),
            pltpu.VMEM((leaves + 1, 128, 128), f32),
            pltpu.VMEM((48, QUAD * 128), bf16),
            pltpu.VMEM((48, QUAD * 128), bf16),
            pltpu.VMEM((128, QUAD * 128), f32),
            pltpu.VMEM((128, QUAD * 128), f32),
        ],
        compiler_params=pltpu.CompilerParams(vmem_limit_bytes=VMEM_LIMIT),
        cost_estimate=pl.CostEstimate(flops=pairs * 96, bytes_accessed=1 << 20, transcendentals=pairs),
        name="near",
    )(counts, sources, offsets, total, data, table)


def count_kernel(blocks, slot_ref, class_ref, out_ref, high, low, held):
    targets, width = slot_ref.shape
    heights = held.shape[0] // targets
    slots = slot_ref[...]
    high[...] = jnp.where(slots >= 0, class_ref[...] * blocks + slots // 128, -1)
    low[...] = jnp.where(slots >= 0, slots % 128, -1)
    high_row = lax.broadcasted_iota(jnp.int32, (heights, width), 0)
    low_row = lax.broadcasted_iota(jnp.int32, (128, width), 0)

    def one(t, carry):
        h = (high_row == high[pl.ds(t, 1), :]).astype(f32).astype(bf16)
        w = (low_row == low[pl.ds(t, 1), :]).astype(f32).astype(bf16)
        held[pl.ds(t, heights, stride=targets), :] = lax.dot_general(h, w, NT, preferred_element_type=f32)
        return carry

    lax.fori_loop(0, targets, one, 0, unroll=4)
    out_ref[...] = held[...].astype(bf16)


def count_call(slots, classes, blocks, operators):
    targets, width = slots.shape
    vmem = pl.BlockSpec(memory_space=pltpu.VMEM)
    rows = operators * blocks * targets
    held = pl.pallas_call(
        functools.partial(count_kernel, blocks),
        out_shape=jax.ShapeDtypeStruct((rows, 128), bf16),
        in_specs=[vmem, vmem],
        out_specs=vmem,
        scratch_shapes=[
            pltpu.VMEM((targets, width), jnp.int32),
            pltpu.VMEM((targets, width), jnp.int32),
            pltpu.VMEM((rows, 128), f32),
        ],
        compiler_params=pltpu.CompilerParams(vmem_limit_bytes=VMEM_LIMIT),
        cost_estimate=pl.CostEstimate(
            flops=targets * 2 * 256 * 128 * operators * blocks, bytes_accessed=rows * 256, transcendentals=0
        ),
        name="count",
    )(slots, classes)
    return held.reshape(operators, blocks, targets, 128)


def far_kernel(
    grands, ids_ref, lc_ref, pc_ref, cc_ref, own_ref, got_ref, pown_ref, pgot_ref, coarse_ref,
    shift_ref, down_ref, pos_ref, chg_ref, self_ref, near_ref, out_ref,
    leaf_src, parent_src, coarse_src, total, wide, spread, held,
):
    o = pl.program_id(0)
    leaves, coef = own_ref.shape
    parents = pown_ref.shape[0]
    coarse = coarse_ref.shape[0]

    @pl.when(o == 0)
    def _():
        total[...] = jnp.zeros_like(total)
        leaf_src[...] = jnp.zeros_like(leaf_src)
        parent_src[...] = jnp.zeros_like(parent_src)
        for target, first, second in ((leaf_src, own_ref, got_ref), (parent_src, pown_ref, pgot_ref)):
            n = first.shape[0]
            for side, half in enumerate(split2(first[...])):
                target[side, :n, :] = half
            for side, half in enumerate(split2(second[...])):
                target[side, n : n + second.shape[0], :] = half
        for side, half in enumerate(split2(coarse_ref[...])):
            coarse_src[side] = half

    def grouped(counts, source):
        lhs = jnp.concatenate([counts[0, b] for b in range(counts.shape[1])], axis=1)
        return jnp.dot(lhs, source[0], preferred_element_type=f32) + jnp.dot(
            lhs, source[1], preferred_element_type=f32
        )

    few = cc_ref[0].astype(bf16)
    small = jnp.dot(few, coarse_src[0], preferred_element_type=f32) + jnp.dot(
        few, coarse_src[1], preferred_element_type=f32
    )
    stacked = jnp.concatenate([grouped(lc_ref, leaf_src), grouped(pc_ref, parent_src), small], axis=0)
    total[...] += dot_nt(stacked, shift_ref[0])

    @pl.when(o == pl.num_programs(0) - 1)
    def _():
        far_parent = total[leaves : leaves + parents, :]
        far_coarse = total[leaves + parents :, :]
        rows = lax.broadcasted_iota(jnp.int32, (coarse, coef), 0)
        grand_rows = []
        for g in range(grands):
            mine = jnp.sum(jnp.where(rows == ids_ref[grands + g], far_coarse, 0.0), axis=0, keepdims=True)
            grand_rows.append(dot_nt(mine, down_ref[ids_ref[g]]))
        grand = jnp.concatenate(grand_rows, axis=0)
        for c in range(8):
            spread_to(spread, pl.ds(c, grands, stride=8), dot_nt(grand, down_ref[c]))
        parent = joined(spread, slice(None), coef) + far_parent
        for c in range(8):
            spread_to(wide, pl.ds(c, parents, stride=8), dot_nt(parent, down_ref[c]))
        loc = joined(wide, slice(None), coef) + total[:leaves, :]
        spread_to(wide, slice(None), loc)
        for b in range(wide.shape[0]):
            held[b * 128 : (b + 1) * 128, :] = wide[b].T
        xt = pos_ref[0].T * 2.0
        yt = pos_ref[1].T * 2.0
        zt = pos_ref[2].T * 2.0
        chunk = 64
        outs = []
        for start in range(0, xt.shape[0], chunk):
            x, y, z = (v[start : start + chunk] for v in (xt, yt, zt))
            pot = None
            for i in range(ORDER, -1, -1):
                mid = None
                for j in range(ORDER - i, -1, -1):
                    low = None
                    for k in range(ORDER - i - j, -1, -1):
                        a = INDEX[(i, j, k)]
                        value = held[a : a + 1, :]
                        low = jnp.broadcast_to(value, x.shape) if low is None else low * z + value
                    mid = low if mid is None else mid * y + low
                pot = mid if pot is None else pot * x + mid
            outs.append(pot)
        far = jnp.concatenate(outs, axis=0)
        alone = self_ref[...] * (1.0 / softening)
        out_ref[...] = (far + near_ref[...] - chg_ref[...].T * alone).T


def far_call(ids, lc, pc, cc, own, got, pown, pgot, coarse, shift, down, pos, chg, alone, near):
    operators, coef = shift.shape[:2]
    leaves, parents, ncoarse = own.shape[0], pown.shape[0], coarse.shape[0]
    vmem = pl.BlockSpec(memory_space=pltpu.VMEM)
    smem = pl.BlockSpec(memory_space=pltpu.SMEM)
    wide = pl.cdiv(coef, 128) * 128

    def per_operator(x):
        return pl.BlockSpec((1,) + x.shape[1:], lambda o: (o,) + (0,) * (x.ndim - 1))

    return pl.pallas_call(
        functools.partial(far_kernel, parents // 8),
        grid=(operators,),
        out_shape=jax.ShapeDtypeStruct((leaves, 128), f32),
        in_specs=[
            smem, per_operator(lc), per_operator(pc), per_operator(cc), vmem, vmem, vmem, vmem, vmem,
            per_operator(shift), vmem, vmem, vmem, vmem, vmem,
        ],
        out_specs=vmem,
        scratch_shapes=[
            pltpu.VMEM((2, lc.shape[1] * 128, coef), bf16),
            pltpu.VMEM((2, pc.shape[1] * 128, coef), bf16),
            pltpu.VMEM((2, ncoarse, coef), bf16),
            pltpu.VMEM((leaves + parents + ncoarse, coef), f32),
            pltpu.VMEM((wide // 128, leaves, 128), f32),
            pltpu.VMEM((wide // 128, parents, 128), f32),
            pltpu.VMEM((wide, leaves), f32),
        ],
        compiler_params=pltpu.CompilerParams(vmem_limit_bytes=VMEM_LIMIT),
        name="far",
    )(ids, lc, pc, cc, own, got, pown, pgot, coarse, shift, down, pos, chg, alone, near)


def per_device(
    positions, charges, near_leaves, near_offsets, far_leaves, far_leaf_class, leaf_plan,
    far_parents, far_parent_class, parent_plan, coarse_lists, coarse_class, up_shift, down_shift, far_shift,
):
    coef = up_shift.shape[1]
    operators = far_shift.shape[0]
    leaves, width = near_leaves.shape
    parents = far_parents.shape[0]
    size = positions.shape[1] // leaves
    ncoarse = coarse_lists.shape[0]
    device = lax.axis_index(AXES)
    devices = lax.axis_size(AXES)
    grands = parents // 8
    grand_ids = device * grands + jnp.arange(grands, dtype=jnp.int32)
    ids = jnp.concatenate([grand_ids % 8, grand_ids // 8])

    pos = positions.reshape(3, leaves, size)
    chg = charges.reshape(leaves, size)

    cap_l, cap_p = leaf_plan.shape[2], parent_plan.shape[2]
    requests = lax.all_to_all(
        jnp.concatenate([leaf_plan, parent_plan], 2), AXES, split_axis=1, concat_axis=0, tiled=True
    )
    asked = jnp.maximum(requests[:, 0, :], 0)

    zero = jnp.zeros((leaves, 1, size), f32)
    data = jnp.concatenate(
        [jnp.moveaxis(pos, 0, 1), zero, zero + 1.0, chg[:, None, :], zero, zero], axis=1
    )
    up = [(i, i + 1) for i in range(devices - 1)]
    down = [(j, i) for i, j in up]
    before = lax.ppermute(data[leaves - RIM :], AXES, up)
    after = lax.ppermute(data[:RIM], AXES, down)

    leaf_rows, parent_rows, lifted = upward_call(ids, pos, chg, up_shift)

    outgoing = jnp.concatenate([leaf_rows[asked[:, :cap_l]], parent_rows[asked[:, cap_l:]]], axis=1)
    arrived = lax.all_to_all(outgoing, AXES, split_axis=0, concat_axis=0, tiled=True)
    member = (
        jnp.arange(ncoarse, dtype=jnp.int32)[:, None] == grand_ids[None, :] // 8
    ).astype(f32)
    coarse = lax.psum(jnp.sum(member[:, :, None] * lifted[None], axis=1), AXES)

    extended = jnp.concatenate([before, data, after, jnp.zeros((1, 8, size), f32)], axis=0)
    present = near_leaves >= 0
    first = device * leaves
    padded = pl.cdiv(width, QUAD) * QUAD
    source = jnp.where(present, near_leaves - first + RIM, leaves + 2 * RIM)
    source = jnp.pad(source, ((0, 1), (0, padded - width)), constant_values=leaves + 2 * RIM).reshape(-1)
    offset = jnp.pad(jnp.where(present, near_offsets, 13), ((0, 1), (0, padded - width)), constant_values=13).reshape(-1)
    counts = jnp.pad(jnp.sum(present.astype(jnp.int32), axis=1), (0, 1))
    total = jnp.sum((counts + QUAD - 1) // QUAD, keepdims=True)
    classes = jnp.arange(27, dtype=jnp.int32)
    shifts = jnp.stack([classes // 9 - 1, classes // 3 % 3 - 1, classes % 3 - 1], axis=1).astype(f32)
    table = jnp.broadcast_to(jnp.pad(shifts, ((0, 0), (0, 5)))[:, :, None], (27, 8, size))
    near = near_call(counts, source, offset, total, extended, table, leaves, padded)
    target_ids = first + jnp.arange(leaves, dtype=jnp.int32)
    alone = jnp.sum(
        ((near_leaves == target_ids[:, None]) & (near_offsets == 13)).astype(f32), axis=1
    )[None, :]

    leaf_blocks = pl.cdiv(leaves + devices * cap_l, 128)
    parent_blocks = pl.cdiv(parents + devices * cap_p, 128)
    lc = count_call(far_leaves, far_leaf_class, leaf_blocks, operators)
    pc = count_call(far_parents, far_parent_class, parent_blocks, operators)
    hit = coarse_class[None] == jnp.arange(operators, dtype=jnp.int32)[:, None, None]
    where = coarse_lists[:, :, None] == jnp.arange(ncoarse, dtype=jnp.int32)
    cc = jnp.sum((hit[..., None] & where[None]).astype(f32), axis=2)
    out = far_call(
        ids, lc, pc, cc, leaf_rows, arrived[:, :cap_l].reshape(-1, coef), parent_rows,
        arrived[:, cap_l:].reshape(-1, coef), coarse, far_shift, down_shift, pos, chg, alone, near,
    )
    return out.reshape(-1)


def solution(mesh):
    one, two, three = P(AXES), P(AXES, None), P(AXES, None, None)
    placed = (
        P(None, AXES), one, two, two, two, two, three, two, two, three, P(), P(), P(), P(), P(),
    )
    return jax.shard_map(per_device, mesh=mesh, in_specs=placed, out_specs=one, check_vma=False)
```

```python
import functools

import jax
import jax.numpy as jnp
from jax import lax
from jax.experimental import pallas as pl
from jax.experimental.pallas import tpu as pltpu
from jax.sharding import PartitionSpec as P

ORDER = 10
RIM = 32
QUAD = 4
GROUP = 4
softening = 0.05
AXES = ("gx", "gy")
VMEM_LIMIT = 56 * 1024 * 1024
f32 = jnp.float32
bf16 = jnp.bfloat16


def exponent_index(order):
    index = {}
    for degree in range(order + 1):
        for i in range(degree, -1, -1):
            for j in range(degree - i, -1, -1):
                index[(i, j, degree - i - j)] = len(index)
    return index


INDEX = exponent_index(ORDER)
NT = (((1,), (1,)), ((), ()))


def split2(x):
    high = x.astype(bf16)
    low = (x - high.astype(f32)).astype(bf16)
    return high, low


def dot_nt(x, w):
    xh, xl = split2(x)
    wh, wl = split2(w)
    out = lax.dot_general(xh, wh, NT, preferred_element_type=f32)
    out += lax.dot_general(xl, wh, NT, preferred_element_type=f32)
    return out + lax.dot_general(xh, wl, NT, preferred_element_type=f32)


def joined(held, rows, coef):
    return jnp.concatenate([held[b, rows, :] for b in range(held.shape[0])], axis=1)[:, :coef]


def spread_to(held, rows, value):
    value = jnp.pad(value, ((0, 0), (0, held.shape[0] * 128 - value.shape[1])))
    for b in range(held.shape[0]):
        held[b, rows, :] = value[:, b * 128 : (b + 1) * 128]


def upward_kernel(ids_ref, pos_ref, chg_ref, up_ref, leaf_ref, parent_ref, lifted_ref, mom, rows, prow, up, sems):
    coef = up.shape[1]
    parents = parent_ref.shape[0]
    grands = parents // 8
    copies = [pltpu.make_async_copy(up_ref.at[:, c, :], up.at[c], sems.at[c]) for c in range(8)]
    for copy in copies:
        copy.start()
    mom[...] = jnp.zeros_like(mom)
    xt = pos_ref[0].T * 2.0
    yt = pos_ref[1].T * 2.0
    zt = pos_ref[2].T * 2.0
    qt = chg_ref[...].T
    size = xt.shape[0]
    chunk = 64
    for start in range(0, size, chunk):
        x, y, z, wi = (v[start : start + chunk] for v in (xt, yt, zt, qt))
        for i in range(ORDER + 1):
            if i:
                wi = wi * x
            wj = wi
            for j in range(ORDER + 1 - i):
                if j:
                    wj = wj * y
                wk = wj
                for k in range(ORDER + 1 - i - j):
                    if k:
                        wk = wk * z
                    a = INDEX[(i, j, k)]
                    mom[a : a + 1, :] += jnp.sum(wk, axis=0, keepdims=True)
    for b in range(mom.shape[0] // 128):
        rows[b] = mom[b * 128 : (b + 1) * 128, :].T
    leaf_ref[...] = joined(rows, slice(None), coef)
    total = jnp.zeros((parents, coef), f32)
    for c in range(8):
        copies[c].wait()
        total += dot_nt(joined(rows, pl.ds(c, parents, stride=8), coef), up[c])
    parent_ref[...] = total
    spread_to(prow, slice(None), total)
    grand = jnp.zeros((grands, coef), f32)
    for c in range(8):
        grand += dot_nt(joined(prow, pl.ds(c, grands, stride=8), coef), up[c])
    for g in range(grands):
        lifted_ref[g : g + 1, :] = dot_nt(grand[g : g + 1], up[ids_ref[g]])


def upward_call(ids, pos, chg, up):
    leaves = pos.shape[1]
    coef = up.shape[0]
    parents = leaves // 8
    wide = pl.cdiv(coef, 128) * 128
    vmem = pl.BlockSpec(memory_space=pltpu.VMEM)
    return pl.pallas_call(
        upward_kernel,
        out_shape=(
            jax.ShapeDtypeStruct((leaves, coef), f32),
            jax.ShapeDtypeStruct((parents, coef), f32),
            jax.ShapeDtypeStruct((parents // 8, coef), f32),
        ),
        in_specs=[pl.BlockSpec(memory_space=pltpu.SMEM), vmem, vmem, pl.BlockSpec(memory_space=pl.ANY)],
        out_specs=(vmem, vmem, vmem),
        scratch_shapes=[
            pltpu.VMEM((wide, leaves), f32),
            pltpu.VMEM((wide // 128, leaves, 128), f32),
            pltpu.VMEM((wide // 128, parents, 128), f32),
            pltpu.VMEM((8, coef, coef), f32),
            pltpu.SemaphoreType.DMA((8,)),
        ],
        compiler_params=pltpu.CompilerParams(vmem_limit_bytes=VMEM_LIMIT),
        name="upward",
    )(ids, pos, chg, up)


def near_kernel(
    leaves, width, count_ref, src_ref, off_ref, total_ref, data_ref, table_ref, shift_ref, out_ref, order_ref,
    targets, acc, sems, *held,
):
    bs, rs = held[:GROUP], held[GROUP:]
    copies = [
        pltpu.make_async_copy(shift_ref.at[:, o, :], order_ref.at[o], sems.at[o])
        for o in range(shift_ref.shape[1])
    ]
    for copy in copies:
        copy.start()
    row = lax.broadcasted_iota(jnp.int32, (8, 128), 0)
    soft = softening * softening

    def pieces(s):
        p1 = s.astype(bf16).astype(f32)
        rest = s - p1
        p2 = rest.astype(bf16).astype(f32)
        return p1, p2, rest - p2

    def set_target(l, carry):
        t = data_ref[RIM + l]
        square = jnp.sum(jnp.where(row < 3, t * t, 0.0), axis=0, keepdims=True)
        t = jnp.where(row < 3, -2.0 * t, jnp.where(row == 3, 1.0, jnp.where(row == 4, square, 0.0)))
        t1, t2, t3 = pieces(t)
        zero = jnp.zeros((80, 128), f32)
        full = jnp.concatenate([t1, t2, t3, t1, t2, t1, zero], axis=0)
        targets[l] = full.T[:, :48].astype(bf16)
        acc[l] = jnp.zeros((128, 128), f32)
        return carry

    lax.fori_loop(0, leaves, set_target, 0, unroll=4)

    def build(l, k, b):
        named = []
        for j in range(QUAD):
            entry = l * width + k + j
            m = src_ref[entry]
            s = data_ref[m] + table_ref[off_ref[entry]]
            square = jnp.sum(jnp.where(row < 3, s * s, 0.0), axis=0, keepdims=True) + soft
            s = jnp.where(row == 3, square, s)
            s1, s2, s3 = pieces(s)
            b[:, j * 128 : (j + 1) * 128] = jnp.concatenate([s1, s1, s1, s2, s2, s3], axis=0).astype(bf16)
            named.append(m)
        return tuple(named)

    def multiply(l, b, r):
        r[...] = jnp.dot(targets[jnp.minimum(l, leaves - 1)], b[...], preferred_element_type=f32)

    def collect(l, named, r):
        charges = [data_ref[m, 5:6, :] for m in named]
        for start in range(0, 128, 32):
            part = acc[l, start : start + 32, :]
            for j in range(QUAD):
                part += lax.rsqrt(r[start : start + 32, j * 128 : (j + 1) * 128]) * charges[j]
            acc[l, start : start + 32, :] = part

    def body(it, state):
        l, k, old, older = state
        for u in range(GROUP):
            collect(older[u][0], older[u][1], rs[u])
        for u in range(GROUP):
            multiply(old[u][0], bs[u], rs[u])
        new = []
        for u in range(GROUP):
            new.append((l, build(l, k, bs[u])))
            more = k + QUAD < count_ref[l]
            k = jnp.where(more, k + QUAD, 0)
            l = jnp.where(more, l, jnp.minimum(l + 1, leaves))
        return l, k, tuple(new), old

    none = ((jnp.int32(leaves), (jnp.int32(data_ref.shape[0] - 1),) * QUAD),) * GROUP
    start = (jnp.int32(0), jnp.int32(0), none, none)
    lax.fori_loop(0, (total_ref[0] + GROUP - 1) // GROUP + 2, body, start)

    lane = lax.broadcasted_iota(jnp.int32, (128, 128), 1)
    out_ref[...] = jnp.zeros_like(out_ref)

    def finish(it, carry):
        out = out_ref[...]
        for u in range(8):
            l = it * 8 + u
            out = jnp.where(lane == l, jnp.sum(acc[l], axis=1, keepdims=True), out)
        out_ref[...] = out
        return carry

    lax.fori_loop(0, leaves // 8, finish, 0)
    for copy in copies:
        copy.wait()


def near_call(counts, sources, offsets, total, data, table, shift, leaves, width):
    vmem = pl.BlockSpec(memory_space=pltpu.VMEM)
    smem = pl.BlockSpec(memory_space=pltpu.SMEM)
    pairs = leaves * 18 * 128 * 128
    return pl.pallas_call(
        functools.partial(near_kernel, leaves, width),
        out_shape=(
            jax.ShapeDtypeStruct((128, leaves), f32),
            jax.ShapeDtypeStruct((shift.shape[1], shift.shape[0], shift.shape[2]), f32),
        ),
        in_specs=[smem, smem, smem, smem, vmem, vmem, pl.BlockSpec(memory_space=pl.ANY)],
        out_specs=(vmem, pl.BlockSpec(memory_space=pl.ANY)),
        scratch_shapes=[
            pltpu.VMEM((leaves, 128, 48), bf16),
            pltpu.VMEM((leaves + 1, 128, 128), f32),
            pltpu.SemaphoreType.DMA((shift.shape[1],)),
        ]
        + [pltpu.VMEM((48, QUAD * 128), bf16)] * GROUP
        + [pltpu.VMEM((128, QUAD * 128), f32)] * GROUP,
        compiler_params=pltpu.CompilerParams(vmem_limit_bytes=VMEM_LIMIT),
        cost_estimate=pl.CostEstimate(flops=pairs * 96, bytes_accessed=1 << 20, transcendentals=pairs),
        name="near",
    )(counts, sources, offsets, total, data, table, shift)


def count_kernel(blocks, slot_ref, class_ref, out_ref, high, low, held):
    targets, width = slot_ref.shape
    heights = held.shape[0] // targets
    slots = slot_ref[...]
    high[...] = jnp.where(slots >= 0, class_ref[...] * blocks + slots // 128, -1)
    low[...] = jnp.where(slots >= 0, slots % 128, -1)
    high_row = lax.broadcasted_iota(jnp.int32, (heights, width), 0)
    low_row = lax.broadcasted_iota(jnp.int32, (128, width), 0)

    def one(t, carry):
        h = (high_row == high[pl.ds(t, 1), :]).astype(f32).astype(bf16)
        w = (low_row == low[pl.ds(t, 1), :]).astype(f32).astype(bf16)
        held[pl.ds(t, heights, stride=targets), :] = lax.dot_general(h, w, NT, preferred_element_type=f32)
        return carry

    lax.fori_loop(0, targets, one, 0, unroll=4)
    out_ref[...] = held[...].astype(bf16)


def count_call(slots, classes, blocks, operators):
    targets, width = slots.shape
    vmem = pl.BlockSpec(memory_space=pltpu.VMEM)
    rows = operators * blocks * targets
    held = pl.pallas_call(
        functools.partial(count_kernel, blocks),
        out_shape=jax.ShapeDtypeStruct((rows, 128), bf16),
        in_specs=[vmem, vmem],
        out_specs=vmem,
        scratch_shapes=[
            pltpu.VMEM((targets, width), jnp.int32),
            pltpu.VMEM((targets, width), jnp.int32),
            pltpu.VMEM((rows, 128), f32),
        ],
        compiler_params=pltpu.CompilerParams(vmem_limit_bytes=VMEM_LIMIT),
        cost_estimate=pl.CostEstimate(
            flops=targets * 2 * 256 * 128 * operators * blocks, bytes_accessed=rows * 256, transcendentals=0
        ),
        name="count",
    )(slots, classes)
    return held.reshape(operators, blocks, targets, 128)


def far_kernel(
    grands, caps, ids_ref, lc_ref, pc_ref, cc_ref, own_ref, pown_ref, got_ref,
    shift_ref, down_ref, pos_ref, chg_ref, self_ref, near_ref, out_ref,
    leaf_src, parent_src, coarse_src, total, wide, spread, held,
    down, sems, parent_rows, lifted_rows,
):
    o = pl.program_id(0)
    leaves, coef = own_ref.shape
    parents = pown_ref.shape[0]
    coarse = coarse_src.shape[1]
    devices = got_ref.shape[0]
    cap_l, cap_p = caps
    copies = [pltpu.make_async_copy(down_ref.at[:, c, :], down.at[c], sems.at[c]) for c in range(8)]

    @pl.when(o == 0)
    def _():
        total[...] = jnp.zeros_like(total)
        for copy in copies:
            copy.start()
        leaf_src[...] = jnp.zeros_like(leaf_src)
        parent_rows[...] = jnp.zeros_like(parent_rows)
        for side, half in enumerate(split2(own_ref[...])):
            leaf_src[side, :leaves, :] = half
        parent_rows[:parents, :] = pown_ref[...]

        for d in range(devices):
            got = got_ref[d]
            first, second = leaves + d * cap_l, parents + d * cap_p
            for side, half in enumerate(split2(got[:cap_l])):
                leaf_src[side, first : first + cap_l, :] = half
            parent_rows[second : second + cap_p, :] = got[cap_l : cap_l + cap_p]
            lifted_rows[d * grands : (d + 1) * grands, :] = got[cap_l + cap_p : cap_l + cap_p + grands]
        for side, half in enumerate(split2(parent_rows[...])):
            parent_src[side] = half
        sums = [jnp.sum(lifted_rows[8 * m : 8 * m + 8, :], axis=0, keepdims=True) for m in range(coarse)]
        for side, half in enumerate(split2(jnp.concatenate(sums, axis=0))):
            coarse_src[side] = half

    def grouped(counts, source):
        lhs = jnp.concatenate([counts[0, b] for b in range(counts.shape[1])], axis=1)
        return jnp.dot(lhs, source[0], preferred_element_type=f32) + jnp.dot(
            lhs, source[1], preferred_element_type=f32
        )

    few = cc_ref[0].astype(bf16)
    small = jnp.dot(few, coarse_src[0], preferred_element_type=f32) + jnp.dot(
        few, coarse_src[1], preferred_element_type=f32
    )
    stacked = jnp.concatenate([grouped(lc_ref, leaf_src), grouped(pc_ref, parent_src), small], axis=0)
    total[...] += dot_nt(stacked, shift_ref[0])

    @pl.when(o == pl.num_programs(0) - 1)
    def _():
        for copy in copies:
            copy.wait()
        far_parent = total[leaves : leaves + parents, :]
        far_coarse = total[leaves + parents :, :]
        rows = lax.broadcasted_iota(jnp.int32, (coarse, coef), 0)
        grand_rows = []
        for g in range(grands):
            mine = jnp.sum(jnp.where(rows == ids_ref[grands + g], far_coarse, 0.0), axis=0, keepdims=True)
            grand_rows.append(dot_nt(mine, down[ids_ref[g]]))
        grand = jnp.concatenate(grand_rows, axis=0)
        for c in range(8):
            spread_to(spread, pl.ds(c, grands, stride=8), dot_nt(grand, down[c]))
        parent = joined(spread, slice(None), coef) + far_parent
        for c in range(8):
            spread_to(wide, pl.ds(c, parents, stride=8), dot_nt(parent, down[c]))
        loc = joined(wide, slice(None), coef) + total[:leaves, :]
        spread_to(wide, slice(None), loc)
        for b in range(wide.shape[0]):
            held[b * 128 : (b + 1) * 128, :] = wide[b].T
        xt = pos_ref[0].T * 2.0
        yt = pos_ref[1].T * 2.0
        zt = pos_ref[2].T * 2.0
        chunk = 64
        outs = []
        for start in range(0, xt.shape[0], chunk):
            x, y, z = (v[start : start + chunk] for v in (xt, yt, zt))
            pot = None
            for i in range(ORDER, -1, -1):
                mid = None
                for j in range(ORDER - i, -1, -1):
                    low = None
                    for k in range(ORDER - i - j, -1, -1):
                        a = INDEX[(i, j, k)]
                        value = held[a : a + 1, :]
                        low = jnp.broadcast_to(value, x.shape) if low is None else low * z + value
                    mid = low if mid is None else mid * y + low
                pot = mid if pot is None else pot * x + mid
            outs.append(pot)
        far = jnp.concatenate(outs, axis=0)
        alone = self_ref[...] * (1.0 / softening)
        out_ref[...] = (far + near_ref[...] - chg_ref[...].T * alone).T


def far_call(caps, ids, lc, pc, cc, own, pown, got, shift, down, pos, chg, alone, near):
    operators, coef = shift.shape[:2]
    leaves, parents, ncoarse = own.shape[0], pown.shape[0], cc.shape[1]
    vmem = pl.BlockSpec(memory_space=pltpu.VMEM)
    smem = pl.BlockSpec(memory_space=pltpu.SMEM)
    wide = pl.cdiv(coef, 128) * 128

    def per_operator(x):
        return pl.BlockSpec((1,) + x.shape[1:], lambda o: (o,) + (0,) * (x.ndim - 1))

    return pl.pallas_call(
        functools.partial(far_kernel, parents // 8, caps),
        grid=(operators,),
        out_shape=jax.ShapeDtypeStruct((leaves, 128), f32),
        in_specs=[
            smem, per_operator(lc), per_operator(pc), per_operator(cc), vmem, vmem, vmem,
            per_operator(shift), pl.BlockSpec(memory_space=pl.ANY), vmem, vmem, vmem, vmem,
        ],
        out_specs=vmem,
        scratch_shapes=[
            pltpu.VMEM((2, lc.shape[1] * 128, coef), bf16),
            pltpu.VMEM((2, pc.shape[1] * 128, coef), bf16),
            pltpu.VMEM((2, ncoarse, coef), bf16),
            pltpu.VMEM((leaves + parents + ncoarse, coef), f32),
            pltpu.VMEM((wide // 128, leaves, 128), f32),
            pltpu.VMEM((wide // 128, parents, 128), f32),
            pltpu.VMEM((wide, leaves), f32),
            pltpu.VMEM((8, coef, coef), f32),
            pltpu.SemaphoreType.DMA((8,)),
            pltpu.VMEM((pc.shape[1] * 128, coef), f32),
            pltpu.VMEM((8 * ncoarse, coef), f32),
        ],
        compiler_params=pltpu.CompilerParams(vmem_limit_bytes=VMEM_LIMIT),
        name="far",
    )(ids, lc, pc, cc, own, pown, got, shift, down, pos, chg, alone, near)


def per_device(
    positions, charges, near_leaves, near_offsets, far_leaves, far_leaf_class, leaf_plan,
    far_parents, far_parent_class, parent_plan, coarse_lists, coarse_class, up_shift, down_shift, far_shift,
):
    coef = up_shift.shape[1]
    operators = far_shift.shape[0]
    leaves, width = near_leaves.shape
    parents = far_parents.shape[0]
    size = positions.shape[1] // leaves
    ncoarse = coarse_lists.shape[0]
    device = lax.axis_index(AXES)
    devices = lax.axis_size(AXES)
    grands = parents // 8
    grand_ids = device * grands + jnp.arange(grands, dtype=jnp.int32)
    ids = jnp.concatenate([grand_ids % 8, grand_ids // 8])

    pos = positions.reshape(3, leaves, size)
    chg = charges.reshape(leaves, size)

    cap_l, cap_p = leaf_plan.shape[2], parent_plan.shape[2]
    requests = lax.all_to_all(
        jnp.concatenate([leaf_plan, parent_plan], 2), AXES, split_axis=1, concat_axis=0, tiled=True
    )
    asked = jnp.maximum(requests[:, 0, :], 0)

    zero = jnp.zeros((leaves, 1, size), f32)
    data = jnp.concatenate(
        [jnp.moveaxis(pos, 0, 1), zero, zero + 1.0, chg[:, None, :], zero, zero], axis=1
    )
    up = [(i, i + 1) for i in range(devices - 1)]
    down = [(j, i) for i, j in up]
    before = lax.ppermute(data[leaves - RIM :], AXES, up)
    after = lax.ppermute(data[:RIM], AXES, down)

    leaf_rows, parent_rows, lifted = upward_call(ids, pos, chg, jnp.swapaxes(up_shift, 0, 1))

    outgoing = jnp.concatenate(
        [
            leaf_rows[asked[:, :cap_l]],
            parent_rows[asked[:, cap_l:]],
            jnp.broadcast_to(lifted[None], (devices,) + lifted.shape),
        ],
        axis=1,
    )
    arrived = lax.all_to_all(outgoing, AXES, split_axis=0, concat_axis=0, tiled=True)

    extended = jnp.concatenate([before, data, after, jnp.zeros((1, 8, size), f32)], axis=0)
    present = near_leaves >= 0
    first = device * leaves
    padded = pl.cdiv(width, QUAD) * QUAD
    source = jnp.where(present, near_leaves - first + RIM, leaves + 2 * RIM)
    source = jnp.pad(source, ((0, 1), (0, padded - width)), constant_values=leaves + 2 * RIM).reshape(-1)
    offset = jnp.pad(jnp.where(present, near_offsets, 13), ((0, 1), (0, padded - width)), constant_values=13).reshape(-1)
    counts = jnp.pad(jnp.sum(present.astype(jnp.int32), axis=1), (0, 1))
    total = jnp.sum((counts + QUAD - 1) // QUAD, keepdims=True)
    classes = jnp.arange(27, dtype=jnp.int32)
    shifts = jnp.stack([classes // 9 - 1, classes // 3 % 3 - 1, classes % 3 - 1], axis=1).astype(f32)
    table = jnp.broadcast_to(jnp.pad(shifts, ((0, 0), (0, 5)))[:, :, None], (27, 8, size))
    near, shifts_by_class = near_call(
        counts, source, offset, total, extended, table, jnp.swapaxes(far_shift, 0, 1), leaves, padded
    )
    target_ids = first + jnp.arange(leaves, dtype=jnp.int32)
    alone = jnp.sum(
        ((near_leaves == target_ids[:, None]) & (near_offsets == 13)).astype(f32), axis=1
    )[None, :]

    leaf_blocks = pl.cdiv(leaves + devices * cap_l, 128)
    parent_blocks = pl.cdiv(parents + devices * cap_p, 128)
    lc = count_call(far_leaves, far_leaf_class, leaf_blocks, operators)
    pc = count_call(far_parents, far_parent_class, parent_blocks, operators)
    hit = coarse_class[None] == jnp.arange(operators, dtype=jnp.int32)[:, None, None]
    where = coarse_lists[:, :, None] == jnp.arange(ncoarse, dtype=jnp.int32)
    cc = jnp.sum((hit[..., None] & where[None]).astype(f32), axis=2)
    out = far_call(
        (cap_l, cap_p), ids, lc, pc, cc, leaf_rows, parent_rows, arrived, shifts_by_class,
        jnp.swapaxes(down_shift, 0, 1), pos, chg, alone, near,
    )
    return out.reshape(-1)


def solution(mesh):
    one, two, three = P(AXES), P(AXES, None), P(AXES, None, None)
    placed = (
        P(None, AXES), one, two, two, two, two, three, two, two, three, P(), P(), P(), P(), P(),
    )
    return jax.shard_map(per_device, mesh=mesh, in_specs=placed, out_specs=one, check_vma=False)
```

```python
import functools

import jax
import jax.numpy as jnp
from jax import lax
from jax.experimental import pallas as pl
from jax.experimental.pallas import tpu as pltpu
from jax.sharding import PartitionSpec as P

ORDER = 10
RIM = 32
QUAD = 4
GROUP = 4
softening = 0.05
AXES = ("gx", "gy")
VMEM_LIMIT = 56 * 1024 * 1024
f32 = jnp.float32
bf16 = jnp.bfloat16


def exponent_index(order):
    index = {}
    for degree in range(order + 1):
        for i in range(degree, -1, -1):
            for j in range(degree - i, -1, -1):
                index[(i, j, degree - i - j)] = len(index)
    return index


INDEX = exponent_index(ORDER)
NT = (((1,), (1,)), ((), ()))


def split2(x):
    high = x.astype(bf16)
    low = (x - high.astype(f32)).astype(bf16)
    return high, low


def dot_nt(x, w):
    xh, xl = split2(x)
    wh, wl = split2(w)
    out = lax.dot_general(xh, wh, NT, preferred_element_type=f32)
    out += lax.dot_general(xl, wh, NT, preferred_element_type=f32)
    return out + lax.dot_general(xh, wl, NT, preferred_element_type=f32)


def joined(held, rows, coef):
    return jnp.concatenate([held[b, rows, :] for b in range(held.shape[0])], axis=1)[:, :coef]


def spread_to(held, rows, value):
    value = jnp.pad(value, ((0, 0), (0, held.shape[0] * 128 - value.shape[1])))
    for b in range(held.shape[0]):
        held[b, rows, :] = value[:, b * 128 : (b + 1) * 128]


def upward_kernel(ids_ref, pos_ref, chg_ref, up_ref, leaf_ref, parent_ref, lifted_ref, mom, rows, prow, up, sems):
    coef = up.shape[1]
    parents = parent_ref.shape[0]
    grands = parents // 8
    copies = [pltpu.make_async_copy(up_ref.at[:, c, :], up.at[c], sems.at[c]) for c in range(8)]
    for copy in copies:
        copy.start()
    mom[...] = jnp.zeros_like(mom)
    xt = pos_ref[0].T * 2.0
    yt = pos_ref[1].T * 2.0
    zt = pos_ref[2].T * 2.0
    qt = chg_ref[...].T
    size = xt.shape[0]
    chunk = 64
    for start in range(0, size, chunk):
        x, y, z, wi = (v[start : start + chunk] for v in (xt, yt, zt, qt))
        for i in range(ORDER + 1):
            if i:
                wi = wi * x
            wj = wi
            for j in range(ORDER + 1 - i):
                if j:
                    wj = wj * y
                wk = wj
                for k in range(ORDER + 1 - i - j):
                    if k:
                        wk = wk * z
                    a = INDEX[(i, j, k)]
                    mom[a : a + 1, :] += jnp.sum(wk, axis=0, keepdims=True)
    for b in range(mom.shape[0] // 128):
        rows[b] = mom[b * 128 : (b + 1) * 128, :].T
    leaf_ref[...] = joined(rows, slice(None), coef)
    total = jnp.zeros((parents, coef), f32)
    for c in range(8):
        copies[c].wait()
        total += dot_nt(joined(rows, pl.ds(c, parents, stride=8), coef), up[c])
    parent_ref[...] = total
    spread_to(prow, slice(None), total)
    grand = jnp.zeros((grands, coef), f32)
    for c in range(8):
        grand += dot_nt(joined(prow, pl.ds(c, grands, stride=8), coef), up[c])
    for g in range(grands):
        lifted_ref[g : g + 1, :] = dot_nt(grand[g : g + 1], up[ids_ref[g]])


def upward_call(ids, pos, chg, up):
    leaves = pos.shape[1]
    coef = up.shape[0]
    parents = leaves // 8
    wide = pl.cdiv(coef, 128) * 128
    vmem = pl.BlockSpec(memory_space=pltpu.VMEM)
    return pl.pallas_call(
        upward_kernel,
        out_shape=(
            jax.ShapeDtypeStruct((leaves, coef), f32),
            jax.ShapeDtypeStruct((parents, coef), f32),
            jax.ShapeDtypeStruct((parents // 8, coef), f32),
        ),
        in_specs=[pl.BlockSpec(memory_space=pltpu.SMEM), vmem, vmem, pl.BlockSpec(memory_space=pl.ANY)],
        out_specs=(vmem, vmem, vmem),
        scratch_shapes=[
            pltpu.VMEM((wide, leaves), f32),
            pltpu.VMEM((wide // 128, leaves, 128), f32),
            pltpu.VMEM((wide // 128, parents, 128), f32),
            pltpu.VMEM((8, coef, coef), f32),
            pltpu.SemaphoreType.DMA((8,)),
        ],
        compiler_params=pltpu.CompilerParams(vmem_limit_bytes=VMEM_LIMIT),
        name="upward",
    )(ids, pos, chg, up)


def near_kernel(
    leaves, width, count_ref, src_ref, off_ref, total_ref, data_ref, table_ref, out_ref,
    targets, acc, *held,
):
    bs, rs = held[:GROUP], held[GROUP:]
    row = lax.broadcasted_iota(jnp.int32, (8, 128), 0)
    soft = softening * softening

    def pieces(s):
        p1 = s.astype(bf16).astype(f32)
        rest = s - p1
        p2 = rest.astype(bf16).astype(f32)
        return p1, p2, rest - p2

    def set_target(l, carry):
        t = data_ref[RIM + l]
        square = jnp.sum(jnp.where(row < 3, t * t, 0.0), axis=0, keepdims=True)
        t = jnp.where(row < 3, -2.0 * t, jnp.where(row == 3, 1.0, jnp.where(row == 4, square, 0.0)))
        t1, t2, t3 = pieces(t)
        zero = jnp.zeros((80, 128), f32)
        full = jnp.concatenate([t1, t2, t3, t1, t2, t1, zero], axis=0)
        targets[l] = full.T[:, :48].astype(bf16)
        acc[l] = jnp.zeros((128, 128), f32)
        return carry

    lax.fori_loop(0, leaves, set_target, 0, unroll=4)

    def build(l, k, b):
        named = []
        for j in range(QUAD):
            entry = l * width + k + j
            m = src_ref[entry]
            s = data_ref[m] + table_ref[off_ref[entry]]
            square = jnp.sum(jnp.where(row < 3, s * s, 0.0), axis=0, keepdims=True) + soft
            s = jnp.where(row == 3, square, s)
            s1, s2, s3 = pieces(s)
            b[:, j * 128 : (j + 1) * 128] = jnp.concatenate([s1, s1, s1, s2, s2, s3], axis=0).astype(bf16)
            named.append(m)
        return tuple(named)

    def multiply(l, b, r):
        r[...] = jnp.dot(targets[jnp.minimum(l, leaves - 1)], b[...], preferred_element_type=f32)

    def collect(l, named, r):
        charges = [data_ref[m, 5:6, :] for m in named]
        for start in range(0, 128, 32):
            part = acc[l, start : start + 32, :]
            for j in range(QUAD):
                part += lax.rsqrt(r[start : start + 32, j * 128 : (j + 1) * 128]) * charges[j]
            acc[l, start : start + 32, :] = part

    def body(it, state):
        l, k, old, older = state
        for u in range(GROUP):
            collect(older[u][0], older[u][1], rs[u])
        for u in range(GROUP):
            multiply(old[u][0], bs[u], rs[u])
        new = []
        for u in range(GROUP):
            new.append((l, build(l, k, bs[u])))
            more = k + QUAD < count_ref[l]
            k = jnp.where(more, k + QUAD, 0)
            l = jnp.where(more, l, jnp.minimum(l + 1, leaves))
        return l, k, tuple(new), old

    none = ((jnp.int32(leaves), (jnp.int32(data_ref.shape[0] - 1),) * QUAD),) * GROUP
    start = (jnp.int32(0), jnp.int32(0), none, none)
    lax.fori_loop(0, (total_ref[0] + GROUP - 1) // GROUP + 2, body, start)

    lane = lax.broadcasted_iota(jnp.int32, (128, 128), 1)
    out_ref[...] = jnp.zeros_like(out_ref)

    def finish(it, carry):
        out = out_ref[...]
        for u in range(8):
            l = it * 8 + u
            out = jnp.where(lane == l, jnp.sum(acc[l], axis=1, keepdims=True), out)
        out_ref[...] = out
        return carry

    lax.fori_loop(0, leaves // 8, finish, 0)


def near_call(counts, sources, offsets, total, data, table, leaves, width):
    vmem = pl.BlockSpec(memory_space=pltpu.VMEM)
    smem = pl.BlockSpec(memory_space=pltpu.SMEM)
    pairs = leaves * 18 * 128 * 128
    return pl.pallas_call(
        functools.partial(near_kernel, leaves, width),
        out_shape=jax.ShapeDtypeStruct((128, leaves), f32),
        in_specs=[smem, smem, smem, smem, vmem, vmem],
        out_specs=vmem,
        scratch_shapes=[
            pltpu.VMEM((leaves, 128, 48), bf16),
            pltpu.VMEM((leaves + 1, 128, 128), f32),
        ]
        + [pltpu.VMEM((48, QUAD * 128), bf16)] * GROUP
        + [pltpu.VMEM((128, QUAD * 128), f32)] * GROUP,
        compiler_params=pltpu.CompilerParams(vmem_limit_bytes=VMEM_LIMIT),
        cost_estimate=pl.CostEstimate(flops=pairs * 96, bytes_accessed=1 << 20, transcendentals=pairs),
        name="near",
    )(counts, sources, offsets, total, data, table)


def count_kernel(blocks, slot_ref, class_ref, out_ref, turned, high, low, held):
    filled, targets = slot_ref.shape
    width = high.shape[1]
    heights = held.shape[0] // targets
    slots = slot_ref[...]
    turned[...] = jnp.full(turned.shape, -1.0, f32)
    turned[:filled, :targets] = jnp.where(slots >= 0, class_ref[...] * blocks + slots // 128, -1).astype(f32)
    high[...] = turned[...].T.astype(jnp.int32)
    turned[:filled, :targets] = jnp.where(slots >= 0, slots % 128, -1).astype(f32)
    low[...] = turned[...].T.astype(jnp.int32)
    high_row = lax.broadcasted_iota(jnp.int32, (heights, width), 0)
    low_row = lax.broadcasted_iota(jnp.int32, (128, width), 0)

    def one(t, carry):
        h = (high_row == high[pl.ds(t, 1), :]).astype(f32).astype(bf16)
        w = (low_row == low[pl.ds(t, 1), :]).astype(f32).astype(bf16)
        held[pl.ds(t, heights, stride=targets), :] = lax.dot_general(h, w, NT, preferred_element_type=f32)
        return carry

    lax.fori_loop(0, targets, one, 0, unroll=8)
    out_ref[...] = held[...].astype(bf16)


def count_call(slots, classes, blocks, operators):
    filled, targets = slots.shape
    width = pl.cdiv(filled, 128) * 128
    vmem = pl.BlockSpec(memory_space=pltpu.VMEM)
    rows = operators * blocks * targets
    held = pl.pallas_call(
        functools.partial(count_kernel, blocks),
        out_shape=jax.ShapeDtypeStruct((rows, 128), bf16),
        in_specs=[vmem, vmem],
        out_specs=vmem,
        scratch_shapes=[
            pltpu.VMEM((width, 128), f32),
            pltpu.VMEM((128, width), jnp.int32),
            pltpu.VMEM((128, width), jnp.int32),
            pltpu.VMEM((rows, 128), f32),
        ],
        compiler_params=pltpu.CompilerParams(vmem_limit_bytes=VMEM_LIMIT),
        cost_estimate=pl.CostEstimate(
            flops=targets * 2 * 256 * 128 * operators * blocks, bytes_accessed=rows * 256, transcendentals=0
        ),
        name="count",
    )(slots, classes)
    return held.reshape(operators, blocks, targets, 128)


def far_kernel(
    grands, caps, ids_ref, lc_ref, pc_ref, cc_ref, own_ref, pown_ref, got_ref,
    shift_ref, down_ref, pos_ref, chg_ref, self_ref, near_ref, out_ref,
    leaf_src, parent_src, coarse_src, total, wide, spread, held,
    down, sems, parent_rows, lifted_rows, shifts, shift_sems,
):
    o = pl.program_id(0)
    leaves, coef = own_ref.shape
    parents = pown_ref.shape[0]
    coarse = coarse_src.shape[1]
    devices = got_ref.shape[0]
    cap_l, cap_p = caps
    operators = shifts.shape[0]
    moves = [
        pltpu.make_async_copy(shift_ref.at[:, i, :], shifts.at[i], shift_sems.at[i]) for i in range(operators)
    ]
    copies = [pltpu.make_async_copy(down_ref.at[:, c, :], down.at[c], sems.at[c]) for c in range(8)]

    @pl.when(o == 0)
    def _():
        total[...] = jnp.zeros_like(total)
        for copy in moves + copies:
            copy.start()
        leaf_src[...] = jnp.zeros_like(leaf_src)
        parent_rows[...] = jnp.zeros_like(parent_rows)
        for side, half in enumerate(split2(own_ref[...])):
            leaf_src[side, :leaves, :] = half
        parent_rows[:parents, :] = pown_ref[...]

        for d in range(devices):
            got = got_ref[d]
            first, second = leaves + d * cap_l, parents + d * cap_p
            for side, half in enumerate(split2(got[:cap_l])):
                leaf_src[side, first : first + cap_l, :] = half
            parent_rows[second : second + cap_p, :] = got[cap_l : cap_l + cap_p]
            lifted_rows[d * grands : (d + 1) * grands, :] = got[cap_l + cap_p : cap_l + cap_p + grands]
        for side, half in enumerate(split2(parent_rows[...])):
            parent_src[side] = half
        sums = [jnp.sum(lifted_rows[8 * m : 8 * m + 8, :], axis=0, keepdims=True) for m in range(coarse)]
        for side, half in enumerate(split2(jnp.concatenate(sums, axis=0))):
            coarse_src[side] = half

    def grouped(counts, source):
        lhs = jnp.concatenate([counts[0, b] for b in range(counts.shape[1])], axis=1)
        return jnp.dot(lhs, source[0], preferred_element_type=f32) + jnp.dot(
            lhs, source[1], preferred_element_type=f32
        )

    few = cc_ref[0].astype(bf16)
    small = jnp.dot(few, coarse_src[0], preferred_element_type=f32) + jnp.dot(
        few, coarse_src[1], preferred_element_type=f32
    )
    stacked = jnp.concatenate([grouped(lc_ref, leaf_src), grouped(pc_ref, parent_src), small], axis=0)
    for i in range(operators):

        @pl.when(o == i)
        def _(i=i):
            moves[i].wait()

    total[...] += dot_nt(stacked, shifts[o])

    @pl.when(o == pl.num_programs(0) - 1)
    def _():
        for copy in copies:
            copy.wait()
        far_parent = total[leaves : leaves + parents, :]
        far_coarse = total[leaves + parents :, :]
        rows = lax.broadcasted_iota(jnp.int32, (coarse, coef), 0)
        grand_rows = []
        for g in range(grands):
            mine = jnp.sum(jnp.where(rows == ids_ref[grands + g], far_coarse, 0.0), axis=0, keepdims=True)
            grand_rows.append(dot_nt(mine, down[ids_ref[g]]))
        grand = jnp.concatenate(grand_rows, axis=0)
        for c in range(8):
            spread_to(spread, pl.ds(c, grands, stride=8), dot_nt(grand, down[c]))
        parent = joined(spread, slice(None), coef) + far_parent
        for c in range(8):
            spread_to(wide, pl.ds(c, parents, stride=8), dot_nt(parent, down[c]))
        loc = joined(wide, slice(None), coef) + total[:leaves, :]
        spread_to(wide, slice(None), loc)
        for b in range(wide.shape[0]):
            held[b * 128 : (b + 1) * 128, :] = wide[b].T
        xt = pos_ref[0].T * 2.0
        yt = pos_ref[1].T * 2.0
        zt = pos_ref[2].T * 2.0
        chunk = 64
        outs = []
        for start in range(0, xt.shape[0], chunk):
            x, y, z = (v[start : start + chunk] for v in (xt, yt, zt))
            pot = None
            for i in range(ORDER, -1, -1):
                mid = None
                for j in range(ORDER - i, -1, -1):
                    low = None
                    for k in range(ORDER - i - j, -1, -1):
                        a = INDEX[(i, j, k)]
                        value = held[a : a + 1, :]
                        low = jnp.broadcast_to(value, x.shape) if low is None else low * z + value
                    mid = low if mid is None else mid * y + low
                pot = mid if pot is None else pot * x + mid
            outs.append(pot)
        far = jnp.concatenate(outs, axis=0)
        alone = self_ref[...] * (1.0 / softening)
        out_ref[...] = (far + near_ref[...] - chg_ref[...].T * alone).T


def far_call(caps, ids, lc, pc, cc, own, pown, got, shift, down, pos, chg, alone, near):
    coef, operators = shift.shape[:2]
    leaves, parents, ncoarse = own.shape[0], pown.shape[0], cc.shape[1]
    vmem = pl.BlockSpec(memory_space=pltpu.VMEM)
    smem = pl.BlockSpec(memory_space=pltpu.SMEM)
    wide = pl.cdiv(coef, 128) * 128

    def per_operator(x):
        return pl.BlockSpec((1,) + x.shape[1:], lambda o: (o,) + (0,) * (x.ndim - 1))

    return pl.pallas_call(
        functools.partial(far_kernel, parents // 8, caps),
        grid=(operators,),
        out_shape=jax.ShapeDtypeStruct((leaves, 128), f32),
        in_specs=[
            smem, per_operator(lc), per_operator(pc), per_operator(cc), vmem, vmem, vmem,
            pl.BlockSpec(memory_space=pl.ANY), pl.BlockSpec(memory_space=pl.ANY), vmem, vmem, vmem, vmem,
        ],
        out_specs=vmem,
        scratch_shapes=[
            pltpu.VMEM((2, lc.shape[1] * 128, coef), bf16),
            pltpu.VMEM((2, pc.shape[1] * 128, coef), bf16),
            pltpu.VMEM((2, ncoarse, coef), bf16),
            pltpu.VMEM((leaves + parents + ncoarse, coef), f32),
            pltpu.VMEM((wide // 128, leaves, 128), f32),
            pltpu.VMEM((wide // 128, parents, 128), f32),
            pltpu.VMEM((wide, leaves), f32),
            pltpu.VMEM((8, coef, coef), f32),
            pltpu.SemaphoreType.DMA((8,)),
            pltpu.VMEM((pc.shape[1] * 128, coef), f32),
            pltpu.VMEM((8 * ncoarse, coef), f32),
            pltpu.VMEM((operators, coef, coef), f32),
            pltpu.SemaphoreType.DMA((operators,)),
        ],
        compiler_params=pltpu.CompilerParams(vmem_limit_bytes=VMEM_LIMIT),
        name="far",
    )(ids, lc, pc, cc, own, pown, got, shift, down, pos, chg, alone, near)


def per_device(
    positions, charges, near_leaves, near_offsets, far_leaves, far_leaf_class, leaf_plan,
    far_parents, far_parent_class, parent_plan, coarse_lists, coarse_class, up_shift, down_shift, far_shift,
):
    coef = up_shift.shape[1]
    operators = far_shift.shape[0]
    leaves, width = near_leaves.shape
    parents = far_parents.shape[0]
    size = positions.shape[1] // leaves
    ncoarse = coarse_lists.shape[0]
    device = lax.axis_index(AXES)
    devices = lax.axis_size(AXES)
    grands = parents // 8
    grand_ids = device * grands + jnp.arange(grands, dtype=jnp.int32)
    ids = jnp.concatenate([grand_ids % 8, grand_ids // 8])

    pos = positions.reshape(3, leaves, size)
    chg = charges.reshape(leaves, size)

    cap_l, cap_p = leaf_plan.shape[2], parent_plan.shape[2]
    requests = lax.all_to_all(
        jnp.concatenate([leaf_plan, parent_plan], 2), AXES, split_axis=1, concat_axis=0, tiled=True
    )
    asked = jnp.maximum(requests[:, 0, :], 0)

    zero = jnp.zeros((leaves, 1, size), f32)
    data = jnp.concatenate(
        [jnp.moveaxis(pos, 0, 1), zero, zero + 1.0, chg[:, None, :], zero, zero], axis=1
    )
    up = [(i, i + 1) for i in range(devices - 1)]
    down = [(j, i) for i, j in up]
    before = lax.ppermute(data[leaves - RIM :], AXES, up)
    after = lax.ppermute(data[:RIM], AXES, down)

    leaf_rows, parent_rows, lifted = upward_call(ids, pos, chg, jnp.swapaxes(up_shift, 0, 1))

    outgoing = jnp.concatenate(
        [
            leaf_rows[asked[:, :cap_l]],
            parent_rows[asked[:, cap_l:]],
            jnp.broadcast_to(lifted[None], (devices,) + lifted.shape),
        ],
        axis=1,
    )
    arrived = lax.all_to_all(outgoing, AXES, split_axis=0, concat_axis=0, tiled=True)

    extended = jnp.concatenate([before, data, after, jnp.zeros((1, 8, size), f32)], axis=0)
    present = near_leaves >= 0
    first = device * leaves
    padded = pl.cdiv(width, QUAD) * QUAD
    source = jnp.where(present, near_leaves - first + RIM, leaves + 2 * RIM)
    source = jnp.pad(source, ((0, 1), (0, padded - width)), constant_values=leaves + 2 * RIM).reshape(-1)
    offset = jnp.pad(jnp.where(present, near_offsets, 13), ((0, 1), (0, padded - width)), constant_values=13).reshape(-1)
    counts = jnp.pad(jnp.sum(present.astype(jnp.int32), axis=1), (0, 1))
    total = jnp.sum((counts + QUAD - 1) // QUAD, keepdims=True)
    classes = jnp.arange(27, dtype=jnp.int32)
    shifts = jnp.stack([classes // 9 - 1, classes // 3 % 3 - 1, classes % 3 - 1], axis=1).astype(f32)
    table = jnp.broadcast_to(jnp.pad(shifts, ((0, 0), (0, 5)))[:, :, None], (27, 8, size))
    near = near_call(counts, source, offset, total, extended, table, leaves, padded)
    target_ids = first + jnp.arange(leaves, dtype=jnp.int32)
    alone = jnp.sum(
        ((near_leaves == target_ids[:, None]) & (near_offsets == 13)).astype(f32), axis=1
    )[None, :]

    leaf_blocks = pl.cdiv(leaves + devices * cap_l, 128)
    parent_blocks = pl.cdiv(parents + devices * cap_p, 128)
    lc = count_call(far_leaves.T, far_leaf_class.T, leaf_blocks, operators)
    pc = count_call(far_parents.T, far_parent_class.T, parent_blocks, operators)
    hit = coarse_class[None] == jnp.arange(operators, dtype=jnp.int32)[:, None, None]
    where = coarse_lists[:, :, None] == jnp.arange(ncoarse, dtype=jnp.int32)
    cc = jnp.sum((hit[..., None] & where[None]).astype(f32), axis=2)
    out = far_call(
        (cap_l, cap_p), ids, lc, pc, cc, leaf_rows, parent_rows, arrived, jnp.swapaxes(far_shift, 0, 1),
        jnp.swapaxes(down_shift, 0, 1), pos, chg, alone, near,
    )
    return out.reshape(-1)


def solution(mesh):
    one, two, three = P(AXES), P(AXES, None), P(AXES, None, None)
    placed = (
        P(None, AXES), one, two, two, two, two, three, two, two, three, P(), P(), P(), P(), P(),
    )
    return jax.shard_map(per_device, mesh=mesh, in_specs=placed, out_specs=one, check_vma=False)
```

```python
import functools

import jax
import jax.numpy as jnp
import numpy as np
from jax import lax
from jax.experimental import pallas as pl
from jax.experimental.pallas import tpu as pltpu
from jax.sharding import PartitionSpec as P

ORDER = 10
RIM = 32
QUAD = 4
GROUP = 4
softening = 0.05
AXES = ("gx", "gy")
VMEM_LIMIT = 56 * 1024 * 1024
f32 = jnp.float32
bf16 = jnp.bfloat16


def exponent_index(order):
    index = {}
    for degree in range(order + 1):
        for i in range(degree, -1, -1):
            for j in range(degree - i, -1, -1):
                index[(i, j, degree - i - j)] = len(index)
    return index


INDEX = exponent_index(ORDER)
NT = (((1,), (1,)), ((), ()))


def split2(x):
    high = x.astype(bf16)
    low = (x - high.astype(f32)).astype(bf16)
    return high, low


def dot_nt(x, w):
    xh, xl = split2(x)
    wh, wl = split2(w)
    out = lax.dot_general(xh, wh, NT, preferred_element_type=f32)
    out += lax.dot_general(xl, wh, NT, preferred_element_type=f32)
    return out + lax.dot_general(xh, wl, NT, preferred_element_type=f32)


def joined(held, rows, coef):
    return jnp.concatenate([held[b, rows, :] for b in range(held.shape[0])], axis=1)[:, :coef]


def spread_to(held, rows, value):
    value = jnp.pad(value, ((0, 0), (0, held.shape[0] * 128 - value.shape[1])))
    for b in range(held.shape[0]):
        held[b, rows, :] = value[:, b * 128 : (b + 1) * 128]


def upward_kernel(ids_ref, pos_ref, chg_ref, up_ref, leaf_ref, parent_ref, lifted_ref, mom, rows, prow, up, sems):
    coef = up.shape[1]
    parents = parent_ref.shape[0]
    grands = parents // 8
    copies = [pltpu.make_async_copy(up_ref.at[:, c, :], up.at[c], sems.at[c]) for c in range(8)]
    for copy in copies:
        copy.start()
    mom[...] = jnp.zeros_like(mom)
    xt = pos_ref[0].T * 2.0
    yt = pos_ref[1].T * 2.0
    zt = pos_ref[2].T * 2.0
    qt = chg_ref[...].T
    size = xt.shape[0]
    chunk = 64
    for start in range(0, size, chunk):
        x, y, z, wi = (v[start : start + chunk] for v in (xt, yt, zt, qt))
        for i in range(ORDER + 1):
            if i:
                wi = wi * x
            wj = wi
            for j in range(ORDER + 1 - i):
                if j:
                    wj = wj * y
                wk = wj
                for k in range(ORDER + 1 - i - j):
                    if k:
                        wk = wk * z
                    a = INDEX[(i, j, k)]
                    mom[a : a + 1, :] += jnp.sum(wk, axis=0, keepdims=True)
    for b in range(mom.shape[0] // 128):
        rows[b] = mom[b * 128 : (b + 1) * 128, :].T
    leaf_ref[...] = joined(rows, slice(None), coef)
    total = jnp.zeros((parents, coef), f32)
    for c in range(8):
        copies[c].wait()
        total += dot_nt(joined(rows, pl.ds(c, parents, stride=8), coef), up[c])
    parent_ref[...] = total
    spread_to(prow, slice(None), total)
    grand = jnp.zeros((grands, coef), f32)
    for c in range(8):
        grand += dot_nt(joined(prow, pl.ds(c, grands, stride=8), coef), up[c])
    for g in range(grands):
        lifted_ref[g : g + 1, :] = dot_nt(grand[g : g + 1], up[ids_ref[g]])


def upward_call(ids, pos, chg, up):
    leaves = pos.shape[1]
    coef = up.shape[0]
    parents = leaves // 8
    wide = pl.cdiv(coef, 128) * 128
    vmem = pl.BlockSpec(memory_space=pltpu.VMEM)
    return pl.pallas_call(
        upward_kernel,
        out_shape=(
            jax.ShapeDtypeStruct((leaves, coef), f32),
            jax.ShapeDtypeStruct((parents, coef), f32),
            jax.ShapeDtypeStruct((parents // 8, coef), f32),
        ),
        in_specs=[pl.BlockSpec(memory_space=pltpu.SMEM), vmem, vmem, pl.BlockSpec(memory_space=pl.ANY)],
        out_specs=(vmem, vmem, vmem),
        scratch_shapes=[
            pltpu.VMEM((wide, leaves), f32),
            pltpu.VMEM((wide // 128, leaves, 128), f32),
            pltpu.VMEM((wide // 128, parents, 128), f32),
            pltpu.VMEM((8, coef, coef), f32),
            pltpu.SemaphoreType.DMA((8,)),
        ],
        compiler_params=pltpu.CompilerParams(vmem_limit_bytes=VMEM_LIMIT),
        name="upward",
    )(ids, pos, chg, up)


def near_kernel(
    leaves, count_ref, entry_ref, total_ref, data_ref, table_ref, out_ref,
    targets, acc, *held,
):
    bs, rs = held[:GROUP], held[GROUP:]
    row = lax.broadcasted_iota(jnp.int32, (8, 128), 0)
    soft = softening * softening

    def pieces(s):
        p1 = s.astype(bf16).astype(f32)
        rest = s - p1
        p2 = rest.astype(bf16).astype(f32)
        return p1, p2, rest - p2

    def set_target(l, carry):
        t = data_ref[RIM + l]
        square = jnp.sum(jnp.where(row < 3, t * t, 0.0), axis=0, keepdims=True)
        t = jnp.where(row < 3, -2.0 * t, jnp.where(row == 3, 1.0, jnp.where(row == 4, square, 0.0)))
        t1, t2, t3 = pieces(t)
        targets[l] = jnp.concatenate([t1, t2, t3, t1, t2, t1], axis=0).T.astype(bf16)
        acc[l] = jnp.zeros((128, 128), f32)
        return carry

    lax.fori_loop(0, leaves, set_target, 0, unroll=4)

    def build(l, k, b):
        named = []
        for j in range(QUAD):
            entry = entry_ref[l, k + j]
            m = lax.shift_right_logical(entry, 5)
            s = data_ref[m] + table_ref[lax.bitwise_and(entry, 31)]
            square = jnp.sum(jnp.where(row < 3, s * s, 0.0), axis=0, keepdims=True) + soft
            s = jnp.where(row == 3, square, s)
            s1, s2, s3 = pieces(s)
            b[:, j * 128 : (j + 1) * 128] = jnp.concatenate([s1, s1, s1, s2, s2, s3], axis=0).astype(bf16)
            named.append(m)
        return tuple(named)

    def multiply(l, b, r):
        r[...] = jnp.dot(targets[jnp.minimum(l, leaves - 1)], b[...], preferred_element_type=f32)

    def collect(l, named, r):
        charges = [data_ref[m, 5:6, :] for m in named]
        for start in range(0, 128, 32):
            part = acc[l, start : start + 32, :]
            for j in range(QUAD):
                part += lax.rsqrt(r[start : start + 32, j * 128 : (j + 1) * 128]) * charges[j]
            acc[l, start : start + 32, :] = part

    def body(it, state):
        l, k, old, older = state
        for u in range(GROUP):
            collect(older[u][0], older[u][1], rs[u])
        for u in range(GROUP):
            multiply(old[u][0], bs[u], rs[u])
        new = []
        for u in range(GROUP):
            new.append((l, build(l, k, bs[u])))
            more = k + QUAD < count_ref[l]
            k = jnp.where(more, k + QUAD, 0)
            l = jnp.where(more, l, jnp.minimum(l + 1, leaves))
        return l, k, tuple(new), old

    none = ((jnp.int32(leaves), (jnp.int32(data_ref.shape[0] - 1),) * QUAD),) * GROUP
    start = (jnp.int32(0), jnp.int32(0), none, none)
    lax.fori_loop(0, (total_ref[0] + GROUP - 1) // GROUP + 2, body, start)

    lane = lax.broadcasted_iota(jnp.int32, (128, 128), 1)
    out_ref[...] = jnp.zeros_like(out_ref)

    def finish(it, carry):
        out = out_ref[...]
        for u in range(8):
            l = it * 8 + u
            out = jnp.where(lane == l, jnp.sum(acc[l], axis=1, keepdims=True), out)
        out_ref[...] = out
        return carry

    lax.fori_loop(0, leaves // 8, finish, 0)


def near_call(counts, entries, total, data, table, leaves):
    vmem = pl.BlockSpec(memory_space=pltpu.VMEM)
    smem = pl.BlockSpec(memory_space=pltpu.SMEM)
    pairs = leaves * 18 * 128 * 128
    return pl.pallas_call(
        functools.partial(near_kernel, leaves),
        out_shape=jax.ShapeDtypeStruct((128, leaves), f32),
        in_specs=[smem, smem, smem, vmem, vmem],
        out_specs=vmem,
        scratch_shapes=[
            pltpu.VMEM((leaves, 128, 48), bf16),
            pltpu.VMEM((leaves + 1, 128, 128), f32),
        ]
        + [pltpu.VMEM((48, QUAD * 128), bf16)] * GROUP
        + [pltpu.VMEM((128, QUAD * 128), f32)] * GROUP,
        compiler_params=pltpu.CompilerParams(vmem_limit_bytes=VMEM_LIMIT),
        cost_estimate=pl.CostEstimate(flops=pairs * 96, bytes_accessed=1 << 20, transcendentals=pairs),
        name="near",
    )(counts, entries, total, data, table)


def count_kernel(blocks, slot_ref, class_ref, out_ref, turned, high, low, held):
    filled, targets = slot_ref.shape
    width = high.shape[1]
    heights = held.shape[0] // targets
    slots = slot_ref[...]
    turned[...] = jnp.full(turned.shape, -1.0, f32)
    turned[:filled, :targets] = jnp.where(slots >= 0, class_ref[...] * blocks + slots // 128, -1).astype(f32)
    high[...] = turned[...].T.astype(jnp.int32)
    turned[:filled, :targets] = jnp.where(slots >= 0, slots % 128, -1).astype(f32)
    low[...] = turned[...].T.astype(jnp.int32)
    high_row = lax.broadcasted_iota(jnp.int32, (heights, width), 0)
    low_row = lax.broadcasted_iota(jnp.int32, (128, width), 0)

    def one(t, carry):
        h = (high_row == high[pl.ds(t, 1), :]).astype(f32).astype(bf16)
        w = (low_row == low[pl.ds(t, 1), :]).astype(f32).astype(bf16)
        held[pl.ds(t, heights, stride=targets), :] = lax.dot_general(h, w, NT, preferred_element_type=f32)
        return carry

    lax.fori_loop(0, targets, one, 0, unroll=8)
    out_ref[...] = held[...].astype(bf16)


def count_call(slots, classes, blocks, operators):
    filled, targets = slots.shape
    width = pl.cdiv(filled, 128) * 128
    vmem = pl.BlockSpec(memory_space=pltpu.VMEM)
    rows = operators * blocks * targets
    held = pl.pallas_call(
        functools.partial(count_kernel, blocks),
        out_shape=jax.ShapeDtypeStruct((rows, 128), bf16),
        in_specs=[vmem, vmem],
        out_specs=vmem,
        scratch_shapes=[
            pltpu.VMEM((width, 128), f32),
            pltpu.VMEM((128, width), jnp.int32),
            pltpu.VMEM((128, width), jnp.int32),
            pltpu.VMEM((rows, 128), f32),
        ],
        compiler_params=pltpu.CompilerParams(vmem_limit_bytes=VMEM_LIMIT),
        cost_estimate=pl.CostEstimate(
            flops=targets * 2 * 256 * 128 * operators * blocks, bytes_accessed=rows * 256, transcendentals=0
        ),
        name="count",
    )(slots, classes)
    return held.reshape(operators, blocks, targets, 128)


def far_kernel(
    grands, caps, ids_ref, lc_ref, pc_ref, cc_ref, own_ref, pown_ref, got_ref,
    shift_ref, down_ref, pos_ref, chg_ref, self_ref, near_ref, out_ref,
    leaf_src, parent_src, coarse_src, total, wide, spread, held,
    down, sems, parent_rows, lifted_rows, shifts, shift_sems,
):
    o = pl.program_id(0)
    leaves, coef = own_ref.shape
    parents = pown_ref.shape[0]
    coarse, across = coarse_src.shape[0], coarse_src.shape[1] // 2
    devices = got_ref.shape[0]
    cap_l, cap_p = caps
    operators = shifts.shape[0]
    moves = [
        pltpu.make_async_copy(shift_ref.at[:, i, :], shifts.at[i], shift_sems.at[i]) for i in range(operators)
    ]
    copies = [pltpu.make_async_copy(down_ref.at[:, c, :], down.at[c], sems.at[c]) for c in range(8)]

    @pl.when(o == 0)
    def _():
        total[...] = jnp.zeros_like(total)
        for copy in moves + copies:
            copy.start()
        for source in (leaf_src, parent_src, coarse_src):
            source[...] = jnp.zeros_like(source)
        parent_rows[...] = jnp.zeros_like(parent_rows)
        for side, half in enumerate(split2(own_ref[...])):
            leaf_src[:leaves, side * across : side * across + coef] = half
        parent_rows[:parents, :] = pown_ref[...]

        for d in range(devices):
            got = got_ref[d]
            first, second = leaves + d * cap_l, parents + d * cap_p
            for side, half in enumerate(split2(got[:cap_l])):
                leaf_src[first : first + cap_l, side * across : side * across + coef] = half
            parent_rows[second : second + cap_p, :] = got[cap_l : cap_l + cap_p]
            lifted_rows[d * grands : (d + 1) * grands, :] = got[cap_l + cap_p : cap_l + cap_p + grands]
        for side, half in enumerate(split2(parent_rows[...])):
            parent_src[:, side * across : side * across + coef] = half
        sums = [jnp.sum(lifted_rows[8 * m : 8 * m + 8, :], axis=0, keepdims=True) for m in range(coarse)]
        for side, half in enumerate(split2(jnp.concatenate(sums, axis=0))):
            coarse_src[:, side * across : side * across + coef] = half

    def added(lhs, source):
        both = jnp.dot(lhs, source[...], preferred_element_type=f32)
        return (both[:, :across] + both[:, across:])[:, :coef]

    def grouped(counts, source):
        lhs = jnp.concatenate([counts[0, b] for b in range(counts.shape[1])], axis=1)
        return added(lhs, source)

    few = cc_ref[0].astype(bf16)
    small = added(few, coarse_src)
    stacked = jnp.concatenate([grouped(lc_ref, leaf_src), grouped(pc_ref, parent_src), small], axis=0)
    for i in range(operators):

        @pl.when(o == i)
        def _(i=i):
            moves[i].wait()

    total[...] += dot_nt(stacked, shifts[o])

    @pl.when(o == pl.num_programs(0) - 1)
    def _():
        for copy in copies:
            copy.wait()
        far_parent = total[leaves : leaves + parents, :]
        far_coarse = total[leaves + parents :, :]
        rows = lax.broadcasted_iota(jnp.int32, (coarse, coef), 0)
        grand_rows = []
        for g in range(grands):
            mine = jnp.sum(jnp.where(rows == ids_ref[grands + g], far_coarse, 0.0), axis=0, keepdims=True)
            grand_rows.append(dot_nt(mine, down[ids_ref[g]]))
        grand = jnp.concatenate(grand_rows, axis=0)
        for c in range(8):
            spread_to(spread, pl.ds(c, grands, stride=8), dot_nt(grand, down[c]))
        parent = joined(spread, slice(None), coef) + far_parent
        for c in range(8):
            spread_to(wide, pl.ds(c, parents, stride=8), dot_nt(parent, down[c]))
        loc = joined(wide, slice(None), coef) + total[:leaves, :]
        spread_to(wide, slice(None), loc)
        for b in range(wide.shape[0]):
            held[b * 128 : (b + 1) * 128, :] = wide[b].T
        xt = pos_ref[0].T * 2.0
        yt = pos_ref[1].T * 2.0
        zt = pos_ref[2].T * 2.0
        chunk = 64
        outs = []
        for start in range(0, xt.shape[0], chunk):
            x, y, z = (v[start : start + chunk] for v in (xt, yt, zt))
            pot = None
            for i in range(ORDER, -1, -1):
                mid = None
                for j in range(ORDER - i, -1, -1):
                    low = None
                    for k in range(ORDER - i - j, -1, -1):
                        a = INDEX[(i, j, k)]
                        value = held[a : a + 1, :]
                        low = jnp.broadcast_to(value, x.shape) if low is None else low * z + value
                    mid = low if mid is None else mid * y + low
                pot = mid if pot is None else pot * x + mid
            outs.append(pot)
        far = jnp.concatenate(outs, axis=0)
        alone = self_ref[...] * (1.0 / softening)
        out_ref[...] = (far + near_ref[...] - chg_ref[...].T * alone).T


def far_call(caps, ids, lc, pc, cc, own, pown, got, shift, down, pos, chg, alone, near):
    coef, operators = shift.shape[:2]
    leaves, parents, ncoarse = own.shape[0], pown.shape[0], cc.shape[1]
    vmem = pl.BlockSpec(memory_space=pltpu.VMEM)
    smem = pl.BlockSpec(memory_space=pltpu.SMEM)
    wide = pl.cdiv(coef, 128) * 128

    def per_operator(x):
        return pl.BlockSpec((1,) + x.shape[1:], lambda o: (o,) + (0,) * (x.ndim - 1))

    return pl.pallas_call(
        functools.partial(far_kernel, parents // 8, caps),
        grid=(operators,),
        out_shape=jax.ShapeDtypeStruct((leaves, 128), f32),
        in_specs=[
            smem, per_operator(lc), per_operator(pc), per_operator(cc), vmem, vmem, vmem,
            pl.BlockSpec(memory_space=pl.ANY), pl.BlockSpec(memory_space=pl.ANY), vmem, vmem, vmem, vmem,
        ],
        out_specs=vmem,
        scratch_shapes=[
            pltpu.VMEM((lc.shape[1] * 128, 2 * wide), bf16),
            pltpu.VMEM((pc.shape[1] * 128, 2 * wide), bf16),
            pltpu.VMEM((ncoarse, 2 * wide), bf16),
            pltpu.VMEM((leaves + parents + ncoarse, coef), f32),
            pltpu.VMEM((wide // 128, leaves, 128), f32),
            pltpu.VMEM((wide // 128, parents, 128), f32),
            pltpu.VMEM((wide, leaves), f32),
            pltpu.VMEM((8, coef, coef), f32),
            pltpu.SemaphoreType.DMA((8,)),
            pltpu.VMEM((pc.shape[1] * 128, coef), f32),
            pltpu.VMEM((8 * ncoarse, coef), f32),
            pltpu.VMEM((operators, coef, coef), f32),
            pltpu.SemaphoreType.DMA((operators,)),
        ],
        compiler_params=pltpu.CompilerParams(vmem_limit_bytes=VMEM_LIMIT),
        name="far",
    )(ids, lc, pc, cc, own, pown, got, shift, down, pos, chg, alone, near)


def per_device(
    positions, charges, near_leaves, near_offsets, far_leaves, far_leaf_class, leaf_plan,
    far_parents, far_parent_class, parent_plan, coarse_lists, coarse_class, up_shift, down_shift, far_shift,
):
    coef = up_shift.shape[1]
    operators = far_shift.shape[0]
    leaves, width = near_leaves.shape
    parents = far_parents.shape[0]
    size = positions.shape[1] // leaves
    ncoarse = coarse_lists.shape[0]
    device = lax.axis_index(AXES)
    devices = lax.axis_size(AXES)
    grands = parents // 8
    grand_ids = device * grands + jnp.arange(grands, dtype=jnp.int32)
    ids = jnp.concatenate([grand_ids % 8, grand_ids // 8])

    pos = positions.reshape(3, leaves, size)
    chg = charges.reshape(leaves, size)

    cap_l, cap_p = leaf_plan.shape[2], parent_plan.shape[2]
    requests = lax.all_to_all(
        jnp.concatenate([leaf_plan, parent_plan], 2), AXES, split_axis=1, concat_axis=0, tiled=True
    )
    asked = jnp.maximum(requests[:, 0, :], 0)

    zero = jnp.zeros((leaves, 1, size), f32)
    data = jnp.concatenate(
        [jnp.moveaxis(pos, 0, 1), zero, zero + 1.0, chg[:, None, :], zero, zero], axis=1
    )
    up = [(i, i + 1) for i in range(devices - 1)]
    down = [(j, i) for i, j in up]
    before = lax.ppermute(data[leaves - RIM :], AXES, up)
    after = lax.ppermute(data[:RIM], AXES, down)

    leaf_rows, parent_rows, lifted = upward_call(ids, pos, chg, jnp.swapaxes(up_shift, 0, 1))

    outgoing = jnp.concatenate(
        [
            leaf_rows[asked[:, :cap_l]],
            parent_rows[asked[:, cap_l:]],
            jnp.broadcast_to(lifted[None], (devices,) + lifted.shape),
        ],
        axis=1,
    )
    arrived = lax.all_to_all(outgoing, AXES, split_axis=0, concat_axis=0, tiled=True)

    extended = jnp.concatenate([before, data, after, jnp.zeros((1, 8, size), f32)], axis=0)
    present = near_leaves >= 0
    first = device * leaves
    padded = pl.cdiv(width, QUAD) * QUAD
    source = jnp.where(present, near_leaves - first + RIM, leaves + 2 * RIM)
    entries = jnp.pad(
        source * 32 + jnp.where(present, near_offsets, 13),
        ((0, 1), (0, padded - width)),
        constant_values=(leaves + 2 * RIM) * 32 + 13,
    )
    counts = jnp.pad(jnp.sum(present.astype(jnp.int32), axis=1), (0, 1))
    total = jnp.sum((counts + QUAD - 1) // QUAD, keepdims=True)
    classes = np.arange(27)
    shifts = np.stack([classes // 9 - 1, classes // 3 % 3 - 1, classes % 3 - 1], axis=1)
    table = np.zeros((27, 8, size), np.float32)
    table[:, :3, :] = shifts[:, :, None]
    near = near_call(counts, entries, total, extended, table, leaves)
    target_ids = first + jnp.arange(leaves, dtype=jnp.int32)
    alone = jnp.sum(
        ((near_leaves == target_ids[:, None]) & (near_offsets == 13)).astype(f32), axis=1
    )[None, :]

    leaf_blocks = pl.cdiv(leaves + devices * cap_l, 128)
    parent_blocks = pl.cdiv(parents + devices * cap_p, 128)
    lc = count_call(far_leaves.T, far_leaf_class.T, leaf_blocks, operators)
    pc = count_call(far_parents.T, far_parent_class.T, parent_blocks, operators)
    hit = coarse_class[None] == jnp.arange(operators, dtype=jnp.int32)[:, None, None]
    where = coarse_lists[:, :, None] == jnp.arange(ncoarse, dtype=jnp.int32)
    cc = jnp.sum((hit[..., None] & where[None]).astype(f32), axis=2)
    out = far_call(
        (cap_l, cap_p), ids, lc, pc, cc, leaf_rows, parent_rows, arrived, jnp.swapaxes(far_shift, 0, 1),
        jnp.swapaxes(down_shift, 0, 1), pos, chg, alone, near,
    )
    return out.reshape(-1)


def solution(mesh):
    one, two, three = P(AXES), P(AXES, None), P(AXES, None, None)
    placed = (
        P(None, AXES), one, two, two, two, two, three, two, two, three, P(), P(), P(), P(), P(),
    )
    return jax.shard_map(per_device, mesh=mesh, in_specs=placed, out_specs=one, check_vma=False)
```

```python
import functools

import jax
import jax.numpy as jnp
import numpy as np
from jax import lax
from jax.experimental import pallas as pl
from jax.experimental.pallas import tpu as pltpu
from jax.sharding import PartitionSpec as P

ORDER = 10
RIM = 32
QUAD = 4
GROUP = 8
softening = 0.05
AXES = ("gx", "gy")
VMEM_LIMIT = 56 * 1024 * 1024
f32 = jnp.float32
bf16 = jnp.bfloat16


def exponent_index(order):
    index = {}
    for degree in range(order + 1):
        for i in range(degree, -1, -1):
            for j in range(degree - i, -1, -1):
                index[(i, j, degree - i - j)] = len(index)
    return index


INDEX = exponent_index(ORDER)
NT = (((1,), (1,)), ((), ()))


def split2(x):
    high = x.astype(bf16)
    low = (x - high.astype(f32)).astype(bf16)
    return high, low


def dot_nt(x, w):
    xh, xl = split2(x)
    wh, wl = split2(w)
    out = lax.dot_general(xh, wh, NT, preferred_element_type=f32)
    out += lax.dot_general(xl, wh, NT, preferred_element_type=f32)
    return out + lax.dot_general(xh, wl, NT, preferred_element_type=f32)


def joined(held, rows, coef):
    return jnp.concatenate([held[b, rows, :] for b in range(held.shape[0])], axis=1)[:, :coef]


def spread_to(held, rows, value):
    value = jnp.pad(value, ((0, 0), (0, held.shape[0] * 128 - value.shape[1])))
    for b in range(held.shape[0]):
        held[b, rows, :] = value[:, b * 128 : (b + 1) * 128]


def upward_kernel(ids_ref, pos_ref, chg_ref, up_ref, leaf_ref, parent_ref, lifted_ref, mom, rows, prow, up, sems):
    coef = up.shape[1]
    parents = parent_ref.shape[0]
    grands = parents // 8
    copies = [pltpu.make_async_copy(up_ref.at[:, c, :], up.at[c], sems.at[c]) for c in range(8)]
    for copy in copies:
        copy.start()
    mom[...] = jnp.zeros_like(mom)
    xt = pos_ref[0].T * 2.0
    yt = pos_ref[1].T * 2.0
    zt = pos_ref[2].T * 2.0
    qt = chg_ref[...].T
    size = xt.shape[0]
    chunk = 64
    for start in range(0, size, chunk):
        x, y, z, wi = (v[start : start + chunk] for v in (xt, yt, zt, qt))
        for i in range(ORDER + 1):
            if i:
                wi = wi * x
            wj = wi
            for j in range(ORDER + 1 - i):
                if j:
                    wj = wj * y
                wk = wj
                for k in range(ORDER + 1 - i - j):
                    if k:
                        wk = wk * z
                    a = INDEX[(i, j, k)]
                    mom[a : a + 1, :] += jnp.sum(wk, axis=0, keepdims=True)
    for b in range(mom.shape[0] // 128):
        rows[b] = mom[b * 128 : (b + 1) * 128, :].T
    leaf_ref[...] = joined(rows, slice(None), coef)
    total = jnp.zeros((parents, coef), f32)
    for c in range(8):
        copies[c].wait()
        total += dot_nt(joined(rows, pl.ds(c, parents, stride=8), coef), up[c])
    parent_ref[...] = total
    spread_to(prow, slice(None), total)
    grand = jnp.zeros((grands, coef), f32)
    for c in range(8):
        grand += dot_nt(joined(prow, pl.ds(c, grands, stride=8), coef), up[c])
    for g in range(grands):
        lifted_ref[g : g + 1, :] = dot_nt(grand[g : g + 1], up[ids_ref[g]])


def upward_call(ids, pos, chg, up):
    leaves = pos.shape[1]
    coef = up.shape[0]
    parents = leaves // 8
    wide = pl.cdiv(coef, 128) * 128
    vmem = pl.BlockSpec(memory_space=pltpu.VMEM)
    return pl.pallas_call(
        upward_kernel,
        out_shape=(
            jax.ShapeDtypeStruct((leaves, coef), f32),
            jax.ShapeDtypeStruct((parents, coef), f32),
            jax.ShapeDtypeStruct((parents // 8, coef), f32),
        ),
        in_specs=[pl.BlockSpec(memory_space=pltpu.SMEM), vmem, vmem, pl.BlockSpec(memory_space=pl.ANY)],
        out_specs=(vmem, vmem, vmem),
        scratch_shapes=[
            pltpu.VMEM((wide, leaves), f32),
            pltpu.VMEM((wide // 128, leaves, 128), f32),
            pltpu.VMEM((wide // 128, parents, 128), f32),
            pltpu.VMEM((8, coef, coef), f32),
            pltpu.SemaphoreType.DMA((8,)),
        ],
        compiler_params=pltpu.CompilerParams(vmem_limit_bytes=VMEM_LIMIT),
        name="upward",
    )(ids, pos, chg, up)


def near_kernel(
    leaves, count_ref, entry_ref, total_ref, data_ref, table_ref, out_ref,
    targets, acc, *held,
):
    bs, rs = held[:GROUP], held[GROUP:]
    row = lax.broadcasted_iota(jnp.int32, (8, 128), 0)
    soft = softening * softening

    def pieces(s):
        p1 = s.astype(bf16).astype(f32)
        rest = s - p1
        p2 = rest.astype(bf16).astype(f32)
        return p1, p2, rest - p2

    def set_target(l, carry):
        t = data_ref[RIM + l]
        square = jnp.sum(jnp.where(row < 3, t * t, 0.0), axis=0, keepdims=True)
        t = jnp.where(row < 3, -2.0 * t, jnp.where(row == 3, 1.0, jnp.where(row == 4, square, 0.0)))
        t1, t2, t3 = pieces(t)
        targets[l] = jnp.concatenate([t1, t2, t3, t1, t2, t1], axis=0).T.astype(bf16)
        acc[l] = jnp.zeros((128, 128), f32)
        return carry

    lax.fori_loop(0, leaves, set_target, 0, unroll=4)

    def build(l, k, b):
        named = []
        for j in range(QUAD):
            entry = entry_ref[l, k + j]
            m = lax.shift_right_logical(entry, 5)
            s = data_ref[m] + table_ref[lax.bitwise_and(entry, 31)]
            square = jnp.sum(jnp.where(row < 3, s * s, 0.0), axis=0, keepdims=True) + soft
            s = jnp.where(row == 3, square, s)
            s1, s2, s3 = pieces(s)
            b[:, j * 128 : (j + 1) * 128] = jnp.concatenate([s1, s1, s1, s2, s2, s3], axis=0).astype(bf16)
            named.append(m)
        return tuple(named)

    def multiply(l, b, r):
        r[...] = jnp.dot(targets[jnp.minimum(l, leaves - 1)], b[...], preferred_element_type=f32)

    def collect(l, named, r):
        charges = [data_ref[m, 5:6, :] for m in named]
        for start in range(0, 128, 32):
            part = acc[l, start : start + 32, :]
            for j in range(QUAD):
                part += lax.rsqrt(r[start : start + 32, j * 128 : (j + 1) * 128]) * charges[j]
            acc[l, start : start + 32, :] = part

    def body(it, state):
        l, k, old, older = state
        for u in range(GROUP):
            collect(older[u][0], older[u][1], rs[u])
        for u in range(GROUP):
            multiply(old[u][0], bs[u], rs[u])
        new = []
        for u in range(GROUP):
            new.append((l, build(l, k, bs[u])))
            more = k + QUAD < count_ref[l]
            k = jnp.where(more, k + QUAD, 0)
            l = jnp.where(more, l, jnp.minimum(l + 1, leaves))
        return l, k, tuple(new), old

    none = ((jnp.int32(leaves), (jnp.int32(data_ref.shape[0] - 1),) * QUAD),) * GROUP
    start = (jnp.int32(0), jnp.int32(0), none, none)
    lax.fori_loop(0, (total_ref[0] + GROUP - 1) // GROUP + 2, body, start)

    lane = lax.broadcasted_iota(jnp.int32, (128, 128), 1)
    out_ref[...] = jnp.zeros_like(out_ref)

    def finish(it, carry):
        out = out_ref[...]
        for u in range(8):
            l = it * 8 + u
            out = jnp.where(lane == l, jnp.sum(acc[l], axis=1, keepdims=True), out)
        out_ref[...] = out
        return carry

    lax.fori_loop(0, leaves // 8, finish, 0)


def near_call(counts, entries, total, data, table, leaves):
    vmem = pl.BlockSpec(memory_space=pltpu.VMEM)
    smem = pl.BlockSpec(memory_space=pltpu.SMEM)
    pairs = leaves * 18 * 128 * 128
    return pl.pallas_call(
        functools.partial(near_kernel, leaves),
        out_shape=jax.ShapeDtypeStruct((128, leaves), f32),
        in_specs=[smem, smem, smem, vmem, vmem],
        out_specs=vmem,
        scratch_shapes=[
            pltpu.VMEM((leaves, 128, 48), bf16),
            pltpu.VMEM((leaves + 1, 128, 128), f32),
        ]
        + [pltpu.VMEM((48, QUAD * 128), bf16)] * GROUP
        + [pltpu.VMEM((128, QUAD * 128), f32)] * GROUP,
        compiler_params=pltpu.CompilerParams(vmem_limit_bytes=VMEM_LIMIT),
        cost_estimate=pl.CostEstimate(flops=pairs * 96, bytes_accessed=1 << 20, transcendentals=pairs),
        name="near",
    )(counts, entries, total, data, table)


def count_kernel(blocks, slot_ref, class_ref, out_ref, turned, high, low, held):
    filled, targets = slot_ref.shape
    width = high.shape[1]
    heights = held.shape[0] // targets
    slots = slot_ref[...]
    turned[...] = jnp.full(turned.shape, -1.0, f32)
    turned[:filled, :targets] = jnp.where(slots >= 0, class_ref[...] * blocks + slots // 128, -1).astype(f32)
    high[...] = turned[...].T.astype(jnp.int32)
    turned[:filled, :targets] = jnp.where(slots >= 0, slots % 128, -1).astype(f32)
    low[...] = turned[...].T.astype(jnp.int32)
    high_row = lax.broadcasted_iota(jnp.int32, (heights, width), 0)
    low_row = lax.broadcasted_iota(jnp.int32, (128, width), 0)

    def one(t, carry):
        h = (high_row == high[pl.ds(t, 1), :]).astype(f32).astype(bf16)
        w = (low_row == low[pl.ds(t, 1), :]).astype(f32).astype(bf16)
        held[pl.ds(t, heights, stride=targets), :] = lax.dot_general(h, w, NT, preferred_element_type=f32)
        return carry

    lax.fori_loop(0, targets, one, 0, unroll=8)
    out_ref[...] = held[...].astype(bf16)


def count_call(slots, classes, blocks, operators):
    filled, targets = slots.shape
    width = pl.cdiv(filled, 128) * 128
    vmem = pl.BlockSpec(memory_space=pltpu.VMEM)
    rows = operators * blocks * targets
    held = pl.pallas_call(
        functools.partial(count_kernel, blocks),
        out_shape=jax.ShapeDtypeStruct((rows, 128), bf16),
        in_specs=[vmem, vmem],
        out_specs=vmem,
        scratch_shapes=[
            pltpu.VMEM((width, 128), f32),
            pltpu.VMEM((128, width), jnp.int32),
            pltpu.VMEM((128, width), jnp.int32),
            pltpu.VMEM((rows, 128), f32),
        ],
        compiler_params=pltpu.CompilerParams(vmem_limit_bytes=VMEM_LIMIT),
        cost_estimate=pl.CostEstimate(
            flops=targets * 2 * 256 * 128 * operators * blocks, bytes_accessed=rows * 256, transcendentals=0
        ),
        name="count",
    )(slots, classes)
    return held.reshape(operators, blocks, targets, 128)


def far_kernel(
    grands, caps, ids_ref, lc_ref, pc_ref, cc_ref, own_ref, pown_ref, got_ref,
    shift_ref, down_ref, pos_ref, chg_ref, self_ref, near_ref, out_ref,
    leaf_src, parent_src, coarse_src, total, wide, spread, held,
    down, sems, parent_rows, lifted_rows, shifts, shift_sems,
):
    o = pl.program_id(0)
    leaves, coef = own_ref.shape
    parents = pown_ref.shape[0]
    coarse, across = coarse_src.shape[0], coarse_src.shape[1] // 2
    devices = got_ref.shape[0]
    cap_l, cap_p = caps
    operators = shifts.shape[0]
    moves = [
        pltpu.make_async_copy(shift_ref.at[:, i, :], shifts.at[i], shift_sems.at[i]) for i in range(operators)
    ]
    copies = [pltpu.make_async_copy(down_ref.at[:, c, :], down.at[c], sems.at[c]) for c in range(8)]

    @pl.when(o == 0)
    def _():
        total[...] = jnp.zeros_like(total)
        for copy in moves + copies:
            copy.start()
        for source in (leaf_src, parent_src, coarse_src):
            source[...] = jnp.zeros_like(source)
        parent_rows[...] = jnp.zeros_like(parent_rows)
        for side, half in enumerate(split2(own_ref[...])):
            leaf_src[:leaves, side * across : side * across + coef] = half
        parent_rows[:parents, :] = pown_ref[...]

        for d in range(devices):
            got = got_ref[d]
            first, second = leaves + d * cap_l, parents + d * cap_p
            for side, half in enumerate(split2(got[:cap_l])):
                leaf_src[first : first + cap_l, side * across : side * across + coef] = half
            parent_rows[second : second + cap_p, :] = got[cap_l : cap_l + cap_p]
            lifted_rows[d * grands : (d + 1) * grands, :] = got[cap_l + cap_p : cap_l + cap_p + grands]
        for side, half in enumerate(split2(parent_rows[...])):
            parent_src[:, side * across : side * across + coef] = half
        sums = [jnp.sum(lifted_rows[8 * m : 8 * m + 8, :], axis=0, keepdims=True) for m in range(coarse)]
        for side, half in enumerate(split2(jnp.concatenate(sums, axis=0))):
            coarse_src[:, side * across : side * across + coef] = half

    def added(lhs, source):
        both = jnp.dot(lhs, source[...], preferred_element_type=f32)
        return (both[:, :across] + both[:, across:])[:, :coef]

    def grouped(counts, source):
        lhs = jnp.concatenate([counts[0, b] for b in range(counts.shape[1])], axis=1)
        return added(lhs, source)

    few = cc_ref[0].astype(bf16)
    small = added(few, coarse_src)
    stacked = jnp.concatenate([grouped(lc_ref, leaf_src), grouped(pc_ref, parent_src), small], axis=0)
    for i in range(operators):

        @pl.when(o == i)
        def _(i=i):
            moves[i].wait()

    total[...] += dot_nt(stacked, shifts[o])

    @pl.when(o == pl.num_programs(0) - 1)
    def _():
        for copy in copies:
            copy.wait()
        far_parent = total[leaves : leaves + parents, :]
        far_coarse = total[leaves + parents :, :]
        rows = lax.broadcasted_iota(jnp.int32, (coarse, coef), 0)
        grand_rows = []
        for g in range(grands):
            mine = jnp.sum(jnp.where(rows == ids_ref[grands + g], far_coarse, 0.0), axis=0, keepdims=True)
            grand_rows.append(dot_nt(mine, down[ids_ref[g]]))
        grand = jnp.concatenate(grand_rows, axis=0)
        for c in range(8):
            spread_to(spread, pl.ds(c, grands, stride=8), dot_nt(grand, down[c]))
        parent = joined(spread, slice(None), coef) + far_parent
        for c in range(8):
            spread_to(wide, pl.ds(c, parents, stride=8), dot_nt(parent, down[c]))
        loc = joined(wide, slice(None), coef) + total[:leaves, :]
        spread_to(wide, slice(None), loc)
        for b in range(wide.shape[0]):
            held[b * 128 : (b + 1) * 128, :] = wide[b].T
        xt = pos_ref[0].T * 2.0
        yt = pos_ref[1].T * 2.0
        zt = pos_ref[2].T * 2.0
        chunk = 64
        outs = []
        for start in range(0, xt.shape[0], chunk):
            x, y, z = (v[start : start + chunk] for v in (xt, yt, zt))
            pot = None
            for i in range(ORDER, -1, -1):
                mid = None
                for j in range(ORDER - i, -1, -1):
                    low = None
                    for k in range(ORDER - i - j, -1, -1):
                        a = INDEX[(i, j, k)]
                        value = held[a : a + 1, :]
                        low = jnp.broadcast_to(value, x.shape) if low is None else low * z + value
                    mid = low if mid is None else mid * y + low
                pot = mid if pot is None else pot * x + mid
            outs.append(pot)
        far = jnp.concatenate(outs, axis=0)
        alone = self_ref[...] * (1.0 / softening)
        out_ref[...] = (far + near_ref[...] - chg_ref[...].T * alone).T


def far_call(caps, ids, lc, pc, cc, own, pown, got, shift, down, pos, chg, alone, near):
    coef, operators = shift.shape[:2]
    leaves, parents, ncoarse = own.shape[0], pown.shape[0], cc.shape[1]
    vmem = pl.BlockSpec(memory_space=pltpu.VMEM)
    smem = pl.BlockSpec(memory_space=pltpu.SMEM)
    wide = pl.cdiv(coef, 128) * 128

    def per_operator(x):
        return pl.BlockSpec((1,) + x.shape[1:], lambda o: (o,) + (0,) * (x.ndim - 1))

    return pl.pallas_call(
        functools.partial(far_kernel, parents // 8, caps),
        grid=(operators,),
        out_shape=jax.ShapeDtypeStruct((leaves, 128), f32),
        in_specs=[
            smem, per_operator(lc), per_operator(pc), per_operator(cc), vmem, vmem, vmem,
            pl.BlockSpec(memory_space=pl.ANY), pl.BlockSpec(memory_space=pl.ANY), vmem, vmem, vmem, vmem,
        ],
        out_specs=vmem,
        scratch_shapes=[
            pltpu.VMEM((lc.shape[1] * 128, 2 * wide), bf16),
            pltpu.VMEM((pc.shape[1] * 128, 2 * wide), bf16),
            pltpu.VMEM((ncoarse, 2 * wide), bf16),
            pltpu.VMEM((leaves + parents + ncoarse, coef), f32),
            pltpu.VMEM((wide // 128, leaves, 128), f32),
            pltpu.VMEM((wide // 128, parents, 128), f32),
            pltpu.VMEM((wide, leaves), f32),
            pltpu.VMEM((8, coef, coef), f32),
            pltpu.SemaphoreType.DMA((8,)),
            pltpu.VMEM((pc.shape[1] * 128, coef), f32),
            pltpu.VMEM((8 * ncoarse, coef), f32),
            pltpu.VMEM((operators, coef, coef), f32),
            pltpu.SemaphoreType.DMA((operators,)),
        ],
        compiler_params=pltpu.CompilerParams(vmem_limit_bytes=VMEM_LIMIT),
        name="far",
    )(ids, lc, pc, cc, own, pown, got, shift, down, pos, chg, alone, near)


def per_device(
    positions, charges, near_leaves, near_offsets, far_leaves, far_leaf_class, leaf_plan,
    far_parents, far_parent_class, parent_plan, coarse_lists, coarse_class, up_shift, down_shift, far_shift,
):
    coef = up_shift.shape[1]
    operators = far_shift.shape[0]
    leaves, width = near_leaves.shape
    parents = far_parents.shape[0]
    size = positions.shape[1] // leaves
    ncoarse = coarse_lists.shape[0]
    device = lax.axis_index(AXES)
    devices = lax.axis_size(AXES)
    grands = parents // 8
    grand_ids = device * grands + jnp.arange(grands, dtype=jnp.int32)
    ids = jnp.concatenate([grand_ids % 8, grand_ids // 8])

    pos = positions.reshape(3, leaves, size)
    chg = charges.reshape(leaves, size)

    cap_l, cap_p = leaf_plan.shape[2], parent_plan.shape[2]
    requests = lax.all_to_all(
        jnp.concatenate([leaf_plan, parent_plan], 2), AXES, split_axis=1, concat_axis=0, tiled=True
    )
    asked = jnp.maximum(requests[:, 0, :], 0)

    zero = jnp.zeros((leaves, 1, size), f32)
    data = jnp.concatenate(
        [jnp.moveaxis(pos, 0, 1), zero, zero + 1.0, chg[:, None, :], zero, zero], axis=1
    )
    up = [(i, i + 1) for i in range(devices - 1)]
    down = [(j, i) for i, j in up]
    before = lax.ppermute(data[leaves - RIM :], AXES, up)
    after = lax.ppermute(data[:RIM], AXES, down)

    leaf_rows, parent_rows, lifted = upward_call(ids, pos, chg, jnp.swapaxes(up_shift, 0, 1))

    outgoing = jnp.concatenate(
        [
            leaf_rows[asked[:, :cap_l]],
            parent_rows[asked[:, cap_l:]],
            jnp.broadcast_to(lifted[None], (devices,) + lifted.shape),
        ],
        axis=1,
    )
    arrived = lax.all_to_all(outgoing, AXES, split_axis=0, concat_axis=0, tiled=True)

    extended = jnp.concatenate([before, data, after, jnp.zeros((1, 8, size), f32)], axis=0)
    present = near_leaves >= 0
    first = device * leaves
    padded = pl.cdiv(width, QUAD) * QUAD
    source = jnp.where(present, near_leaves - first + RIM, leaves + 2 * RIM)
    entries = jnp.pad(
        source * 32 + jnp.where(present, near_offsets, 13),
        ((0, 1), (0, padded - width)),
        constant_values=(leaves + 2 * RIM) * 32 + 13,
    )
    counts = jnp.pad(jnp.sum(present.astype(jnp.int32), axis=1), (0, 1))
    total = jnp.sum((counts + QUAD - 1) // QUAD, keepdims=True)
    classes = np.arange(27)
    shifts = np.stack([classes // 9 - 1, classes // 3 % 3 - 1, classes % 3 - 1], axis=1)
    table = np.zeros((27, 8, size), np.float32)
    table[:, :3, :] = shifts[:, :, None]
    near = near_call(counts, entries, total, extended, table, leaves)
    target_ids = first + jnp.arange(leaves, dtype=jnp.int32)
    alone = jnp.sum(
        ((near_leaves == target_ids[:, None]) & (near_offsets == 13)).astype(f32), axis=1
    )[None, :]

    leaf_blocks = pl.cdiv(leaves + devices * cap_l, 128)
    parent_blocks = pl.cdiv(parents + devices * cap_p, 128)
    lc = count_call(far_leaves.T, far_leaf_class.T, leaf_blocks, operators)
    pc = count_call(far_parents.T, far_parent_class.T, parent_blocks, operators)
    hit = coarse_class[None] == jnp.arange(operators, dtype=jnp.int32)[:, None, None]
    where = coarse_lists[:, :, None] == jnp.arange(ncoarse, dtype=jnp.int32)
    cc = jnp.sum((hit[..., None] & where[None]).astype(f32), axis=2)
    out = far_call(
        (cap_l, cap_p), ids, lc, pc, cc, leaf_rows, parent_rows, arrived, jnp.swapaxes(far_shift, 0, 1),
        jnp.swapaxes(down_shift, 0, 1), pos, chg, alone, near,
    )
    return out.reshape(-1)


def solution(mesh):
    one, two, three = P(AXES), P(AXES, None), P(AXES, None, None)
    placed = (
        P(None, AXES), one, two, two, two, two, three, two, two, three, P(), P(), P(), P(), P(),
    )
    return jax.shard_map(per_device, mesh=mesh, in_specs=placed, out_specs=one, check_vma=False)
```
